32 devices in a mesh: grp: 2 (over y), row: 4 (over z), ch: 4 (over x, core).
Axes of the slice: x: 2, y: 2, z: 4, core: 2. Of those that a mesh axis runs over, the one named last changes fastest.
Arguments:
- pair: bfloat16 [112, 56, 128], P(('grp', 'row')), parts along dimension 0, may hold values from -6 to 6
- chain_ids: int32 [112], P('grp'), parts along dimension 0, may hold values from 0 to 5, never falling along the last dimension, each value on 1 to 18 neighbouring positions
- mask: int32 [112, 56], P(('grp', 'row')), parts along dimension 0, may hold values 0 or 1
- pair_embed: float32 [2, 128], replicated, may hold values from -6 to 6
- in_gain: float32 [2, 128], replicated, may hold values from 0.5 to 1.5
- in_bias: float32 [2, 128], replicated, may hold values from -3 to 3
- proj_weight: bfloat16 [2, 4, 128, 128], P(None, None, None, 'ch'), may hold values from -0.5 to 0.5
- gate_weight: bfloat16 [2, 128, 128], replicated, may hold values from -0.5 to 0.5
- out_gain: float32 [2, 128], replicated, may hold values from 0.5 to 1.5
- out_bias: float32 [2, 128], replicated, may hold values from -3 to 3
- out_weight: bfloat16 [2, 128, 128], replicated, may hold values from -0.5 to 0.5
Outputs:
- pair_out: bfloat16 [112, 56, 128], P(('grp', 'row')), parts along dimension 0
The draws below stay inside these ranges and needn't reach their ends.
There are 2 independent parts, one for each index of `grp`. The reference program is written for one: setup_inputs(seed, part) draws one part's arguments, and reference() takes and returns one part's arrays. A program takes and returns all parts, laid end to end along the dimension named above; an argument that names none is the same for every part. Nothing has to cross between parts.
Inputs may be any that keep to these rules, and one draw needn't show every extreme that they name: `chain_ids`: chain numbers never fall along the residues; each chain has 1 to 18 residues.
All inputs are finite; a program needn't handle non-finite values. No bound on the sum of `mask` on one device may be relied on, other than what follows from the above.
Results may differ from the reference program's by a relative error of at most 0.008.
Values may be sent and summed in bfloat16 or wider, within the bound.
No kernel may reach another device: no remote copies, remote signals or barrier semaphores. Data moves between devices by JAX's collectives and lax.ppermute only.
A program may use at most 128 MiB of HBM per device.

```python
import math
import jax
import jax.numpy as jnp
import numpy as np
from jax import lax

C = 128
H = 128
CHAINS = 6
N = 56


def place_ends(entries, key, low, largest):
    shape = entries.shape
    index_at = [jax.random.randint(jax.random.fold_in(key, axis), (), 0, shape[axis]) for axis in range(len(shape))]
    entries = entries.at[tuple(index_at)].set(low)
    longest = shape.index(max(shape))
    index_at[longest] = (index_at[longest] + 1) % shape[longest]
    return entries.at[tuple(index_at)].set(largest)


def steps_of(stream_key, extent, pieces, least, top_value):
    level, own = 1.0, jax.random.fold_in(stream_key, 6)
    for axis_at, blocks in pieces:
        heights = jnp.exp(jax.random.uniform(jax.random.fold_in(own, axis_at), (blocks,), jnp.float32, least / len(pieces), top_value / len(pieces)))
        level = level * jnp.repeat(heights, extent[axis_at] // blocks).reshape([-1 if axis == axis_at else 1 for axis in range(len(extent))])
    return level


def split_up(count, total, reach, slope):
    loads = [(1 << 20) // math.isqrt(rank ** slope) + 1 for rank in range(2, count + 1)]
    surplus, counts = total - reach - (count - 1), [1] * (count - 1)
    while surplus > 0:
        candidates = [i for i in range(count - 1) if counts[i] < reach]
        whole, remaining = sum([loads[i] for i in candidates]), surplus
        for i in candidates:
            addition = min(reach - counts[i], max(1, remaining * loads[i] // whole), surplus)
            counts[i] = counts[i] + addition
            surplus = surplus - addition
    return np.array([reach] + counts)


def uneven(key, number_of, total, reach, slope):
    if number_of == 2:
        one = jax.random.randint(key, (), max(1, total - reach), min(reach, total - 1) + 1)
        return jnp.stack([one, total - one])
    lengths = jnp.asarray(split_up(number_of, total, reach, slope), jnp.int32)
    pairs = (number_of - 1) // 2
    donor, sink = lengths[1:1 + 2 * pairs:2], lengths[2:2 + 2 * pairs:2]
    room = jnp.minimum(donor - 1, reach - sink)
    passed = jax.random.randint(jax.random.fold_in(key, 1), (pairs,), 0, 1 << 20) % (room + 1)
    lengths = lengths.at[1:1 + 2 * pairs:2].set(donor - passed).at[2:2 + 2 * pairs:2].set(sink + passed)
    return lengths[jax.random.permutation(jax.random.fold_in(key, 2), number_of)]


def normal_values(own_key, shape, scale, reach, pieces=(), kind=jnp.bfloat16):
    drawn = scale * jax.random.normal(own_key, shape, jnp.float32)
    if pieces:
        drawn = drawn * steps_of(own_key, shape, pieces, -0.22, 0.18)
    return jnp.clip(drawn, -reach, reach).astype(kind)


def setup_inputs(seed: int = 0, part: int = 0) -> dict:
    splits = jax.random.split(jax.random.key(seed), 12)
    own_keys = jax.random.split(jax.random.fold_in(splits[11], part), 12)
    return {
        "pair": normal_values(own_keys[0], (N, N, C), 1.0, 6.0, ((0, 4),)),
        "chain_ids": jnp.searchsorted(jnp.cumsum(uneven(own_keys[1], CHAINS, N, N // 3, 1)), jnp.arange(N), side="right").astype(jnp.int32),
        "mask": place_ends((jax.random.randint(own_keys[2], (N, N), 0, 8) < 7).astype(jnp.int32), jax.random.fold_in(own_keys[2], 1), 0, 1),
        "pair_embed": normal_values(splits[3], (2, C), 1.0, 6.0, (), jnp.float32),
        "in_gain": jnp.clip(1.0 + 0.1 * jax.random.normal(splits[4], (2, C), jnp.float32), 0.5, 1.5),
        "in_bias": normal_values(splits[5], (2, C), 0.3, 3.0, (), jnp.float32),
        "proj_weight": normal_values(splits[6], (2, 4, C, H), C ** -0.5, 0.5, ((3, 4),)),
        "gate_weight": normal_values(splits[7], (2, C, C), C ** -0.5, 0.5),
        "out_gain": jnp.clip(1.0 + 0.1 * jax.random.normal(splits[8], (2, H), jnp.float32), 0.5, 1.5),
        "out_bias": normal_values(splits[9], (2, H), 0.3, 3.0, (), jnp.float32),
        "out_weight": normal_values(splits[10], (2, H, C), H ** -0.5, 0.5),
    }


EPS = 1e-05

def layer_norm(values, gain, bias):
    mean = lax.optimization_barrier(jnp.mean(values, axis=-1, keepdims=True))
    centered = values - mean
    var = lax.optimization_barrier(jnp.mean(centered * centered, axis=-1, keepdims=True))
    return centered * jax.lax.rsqrt(var + EPS) * gain + bias

def gated(normed, weights, maskf):
    gate = jnp.einsum('ijc,ch->hij', normed, weights[0].astype(jnp.float32))
    value = jnp.einsum('ijc,ch->hij', normed, weights[1].astype(jnp.float32))
    return (jax.nn.sigmoid(gate) * value * maskf).astype(jnp.bfloat16)

def one_update(current, layer, maskf, in_gain, in_bias, proj_weight, gate_weight, out_gain, out_bias, out_weight):
    normed = layer_norm(current, in_gain[layer], in_bias[layer]).astype(jnp.bfloat16)
    normf = normed.astype(jnp.float32)
    left = gated(normf, proj_weight[layer, 0:2], maskf).astype(jnp.float32)
    right = gated(normf, proj_weight[layer, 2:4], maskf).astype(jnp.float32)
    if layer == 0:
        mixed = jnp.einsum('hik,hjk->hij', left, right)
    else:
        mixed = jnp.einsum('hki,hkj->hij', left, right)
    values = mixed.astype(jnp.bfloat16).astype(jnp.float32)
    mean = lax.optimization_barrier(jnp.mean(values, axis=0))
    meansq = lax.optimization_barrier(jnp.mean(values * values, axis=0))
    scale = jax.lax.rsqrt(meansq - mean * mean + EPS)
    hidden = ((values - mean) * scale * out_gain[layer][:, None, None] + out_bias[layer][:, None, None]).astype(jnp.bfloat16)
    update = jnp.einsum('hij,hc->ijc', hidden.astype(jnp.float32), out_weight[layer].astype(jnp.float32))
    gate = jax.nn.sigmoid(jnp.einsum('ijd,dc->ijc', normf, gate_weight[layer].astype(jnp.float32)))
    return current + gate * update

def reference(pair, chain_ids, mask, pair_embed, in_gain, in_bias, proj_weight, gate_weight, out_gain, out_bias, out_weight):
    same = (chain_ids[:, None] == chain_ids[None, :])[:, :, None]
    current = pair.astype(jnp.float32) + jnp.where(same, pair_embed[1], pair_embed[0])
    maskf = mask.astype(jnp.float32)
    first = one_update(current, 0, maskf, in_gain, in_bias, proj_weight, gate_weight, out_gain, out_bias, out_weight)
    stored = jax.lax.optimization_barrier(first.astype(jnp.bfloat16))
    second = one_update(stored.astype(jnp.float32), 1, maskf, in_gain, in_bias, proj_weight, gate_weight, out_gain, out_bias, out_weight)
    return second.astype(jnp.bfloat16)
```

```python
import functools

import jax
import jax.numpy as jnp
from jax import lax
from jax.experimental import pallas as pl
from jax.experimental.pallas import tpu as pltpu
from jax.sharding import PartitionSpec as P

EPS = 1e-05
F32 = jnp.float32
BF16 = jnp.bfloat16
MASK_ROWS = 16


def nt_dot(a, b):
    return lax.dot_general(a, b, (((1,), (1,)), ((), ())), preferred_element_type=F32)


def nn_dot(a, b):
    return lax.dot_general(a, b, (((1,), (0,)), ((), ())), preferred_element_type=F32)


def half_sigmoid(half):
    return 0.5 * jnp.tanh(half) + 0.5


def normalize(values, gain, bias):
    mean = jnp.mean(values, axis=-1, keepdims=True)
    centered = values - mean
    var = jnp.mean(centered * centered, axis=-1, keepdims=True)
    return (centered * lax.rsqrt(var + EPS) * gain + bias).astype(BF16)


def pieces(rows, most):
    out, first = [], 0
    while first < rows:
        count = min(most, rows - first)
        out.append((first, count))
        first += count
    return out


def pack_kernel(n, rows, half, pair, mask, weights, packed, halved):
    core = lax.rem(lax.axis_index("ch"), 2)
    block = rows * n
    chan = pair.shape[1]
    masks = jnp.concatenate([mask[...].astype(F32), jnp.zeros((rows, chan - n), F32)], axis=1)
    masks = jnp.concatenate([masks, jnp.zeros((MASK_ROWS - rows, chan), F32)], axis=0).astype(BF16)
    size = weights.shape[0]
    packed[0:block, :] = pair[...]
    packed[block : block + size, :] = weights[...]
    packed[block + size : block + size + MASK_ROWS, :] = masks
    start = pl.multiple_of(core * (rows - half) * n, 16)
    halved[0 : half * n, :] = pair[pl.ds(start, half * n), :]
    halved[half * n : half * n + MASK_ROWS, :] = masks


def whole_kernel(
    n,
    rows,
    half,
    packed_o, packed_a, packed_e, half_b, half_f, w_e,
    chain_s, chain_v, embed, in_gain, in_bias, gate_w, out_gain, out_bias, out_w,
    result,
    z_ref, zn_ref, zm_ref, mask_ref, left_ref, right_ref, x_ref, w_ref,
):
    r = lax.axis_index("row")
    c = lax.axis_index("ch")
    core = lax.rem(c, 2)
    block = rows * n
    chan = packed_o.shape[1]
    size = w_e.shape[0]
    hid = size // 8
    masks_at = block + size

    def put_weights(ref, at, position):
        for u in range(2):
            for q in range(4):
                first = at + (u * 4 + q) * hid
                w_ref[u, q, position] = ref[first : first + hid, :] * jnp.asarray(0.5, BF16)

    put_weights(packed_o, block, c)
    put_weights(w_e, 0, c ^ 1)
    put_weights(packed_a, block, c ^ 2)
    put_weights(packed_e, block, c ^ 3)

    chains = jnp.broadcast_to(chain_v[...], (n, chan))
    gain0, bias0 = in_gain[0:1, :], in_bias[0:1, :]
    other, same = embed[0:1, :], embed[1:2, :]

    spread = (
        lax.broadcasted_iota(jnp.int32, (MASK_ROWS, rows * chan), 1) // chan
        == lax.broadcasted_iota(jnp.int32, (MASK_ROWS, rows * chan), 0)
    ).astype(BF16)

    def load_rows(pair, pair_at, position, first, count, masks):
        z = jnp.concatenate(
            [
                jnp.where(chains == chain_s[position * rows + i], same, other)
                for i in range(first, first + count)
            ],
            axis=0,
        ) + pair[pair_at : pair_at + count * n, :].astype(F32)
        zn = normalize(z, gain0, bias0)
        spread_mask = jnp.concatenate(
            [masks[:, i * chan : (i + 1) * chan] for i in range(first, first + count)], axis=0
        ).astype(BF16)
        at = pl.ds(pl.multiple_of(position * block + first * n, 16), count * n)
        z_ref[at, :] = z
        zn_ref[at, :] = zn
        mask_ref[at, :] = spread_mask
        zm_ref[at, :] = zn * spread_mask

    def spread_masks(ref, at):
        masks = ref[at : at + MASK_ROWS, 0:n]
        return lax.dot_general(masks, spread, (((0,), (0,)), ((), ())), preferred_element_type=F32)

    def load_block(ref, position):
        masks = spread_masks(ref, masks_at)
        for first, count in pieces(rows, 8):
            load_rows(ref, first * n, position, first, count, masks)

    load_block(packed_o, r)
    load_block(packed_a, r ^ (1 + core))
    load_block(packed_e, r ^ (2 - core))
    masks = spread_masks(half_b, half * n)
    rest = rows - half

    @pl.when(core == 0)
    def _():
        load_rows(half_b, 0, r ^ 3, 0, half, masks)
        load_rows(half_f, (half - rest) * n, r ^ 3, half, rest, masks)

    @pl.when(core == 1)
    def _():
        load_rows(half_f, 0, r ^ 3, 0, half, masks)
        load_rows(half_b, (half - rest) * n, r ^ 3, half, rest, masks)

    many = 8

    def project(u, transposed_right):
        weights = [w_ref[u, q].reshape(4 * hid, chan) for q in range(4)]

        def some(t, _):
            at = pl.ds(pl.multiple_of(t * many * n, 16), many * n)
            zm = zm_ref[at, :]
            left_ref[at, :] = (jnp.tanh(nt_dot(zm, weights[0])) + 1.0) * nt_dot(zm, weights[1])
            right = (jnp.tanh(nt_dot(zm, weights[2])) + 1.0) * nt_dot(zm, weights[3])
            if transposed_right:
                for k in range(many):
                    right_ref[pl.ds(many * t + k, n, stride=n), :] = right[k * n : (k + 1) * n]
            else:
                right_ref[at, :] = right
            return 0

        lax.fori_loop(0, n // many, some, 0)

    def triangle(count, left_at, step, out_at):
        def body(k, accs):
            right = right_ref[pl.ds(pl.multiple_of(k * n, 8), n), :]
            return tuple(
                acc + left_ref[pl.ds(left_at(i) + k * step, 1), :] * right for i, acc in enumerate(accs)
            )

        accs = lax.fori_loop(0, n, body, tuple(jnp.zeros((n, chan), F32) for _ in range(count)), unroll=8)
        for i, acc in enumerate(accs):
            x_ref[pl.ds(pl.multiple_of(out_at + i * n, 8), n), :] = acc

    def finish(u, x_at, z_at, size):
        x = x_ref[pl.ds(x_at, size), :]
        mean = jnp.mean(x, axis=-1, keepdims=True)
        meansq = jnp.mean(x * x, axis=-1, keepdims=True)
        scale = lax.rsqrt(meansq - mean * mean + EPS)
        hidden = ((x - mean) * scale * out_gain[u : u + 1, :] + out_bias[u : u + 1, :]).astype(BF16)
        update = nn_dot(hidden, out_w[u])
        gate = jax.nn.sigmoid(nn_dot(zn_ref[pl.ds(z_at, size), :], gate_w[u]))
        return z_ref[pl.ds(z_at, size), :] + gate * update

    project(0, True)
    group = 4

    def some_rows(t, _):
        triangle(group, lambda i: (t * group + i) * n, 1, t * group * n)
        return 0

    lax.fori_loop(0, n // group, some_rows, 0)

    def first_finish(t, _):
        at = pl.multiple_of(t * many * n, 16)
        z1 = finish(0, at, at, many * n).astype(BF16).astype(F32)
        where = pl.ds(at, many * n)
        z_ref[where, :] = z1
        zn = normalize(z1, in_gain[1:2, :], in_bias[1:2, :])
        zn_ref[where, :] = zn
        zm_ref[where, :] = zn * mask_ref[where, :]
        return 0

    lax.fori_loop(0, n // many, first_finish, 0)

    project(1, False)
    start = r * rows
    for first, count in pieces(rows, group):
        triangle(count, lambda i: start + first + i, n, first * n)
    for first, count in pieces(rows, 8):
        out = finish(1, first * n, pl.multiple_of(r * block + first * n, 16), count * n)
        for i in range(count):
            result[first + i] = out[i * n : (i + 1) * n].astype(BF16)


def in_one_phase(
    pair, chain_ids, mask, pair_embed, in_gain, in_bias, proj_weight, gate_weight, out_gain, out_bias, out_weight
):
    rows, n, chan = pair.shape
    hid = proj_weight.shape[3]
    size = 8 * hid
    weights = jnp.transpose(proj_weight, (0, 1, 3, 2)).reshape(size, chan)
    half = (rows // 2 + 1) // 2 * 2
    both = ("row", "ch")
    vmem = pl.BlockSpec(memory_space=pltpu.VMEM)
    smem = pl.BlockSpec(memory_space=pltpu.SMEM)

    def pairs_of(source):
        return [(source(r, c), r * 4 + c) for r in range(4) for c in range(4)]

    first = pairs_of(lambda r, c: (r ^ (1 + c % 2)) * 4 + (c ^ 2))
    second = pairs_of(lambda r, c: (r ^ 3) * 4 + c)
    cores = [(c, c ^ 1) for c in range(4)]

    packed, halved = pl.pallas_call(
        functools.partial(pack_kernel, n, rows, half),
        out_shape=(
            jax.ShapeDtypeStruct((rows * n + size + MASK_ROWS, chan), BF16),
            jax.ShapeDtypeStruct((half * n + MASK_ROWS, chan), BF16),
        ),
        in_specs=[vmem] * 3,
        out_specs=(vmem, vmem),
        name="pack",
    )(pair.reshape(rows * n, chan), mask, weights)
    packed_a = lax.ppermute(packed, both, first)
    half_b = lax.ppermute(halved, both, second)
    w_e = lax.ppermute(weights, "ch", cores)
    packed_e = lax.ppermute(packed_a, "ch", cores)
    half_f = lax.ppermute(half_b, "ch", cores)

    flat = n * n
    return pl.pallas_call(
        functools.partial(whole_kernel, n, rows, half),
        out_shape=jax.ShapeDtypeStruct((rows, n, chan), BF16),
        in_specs=[vmem] * 6 + [smem] + [vmem] * 8,
        out_specs=vmem,
        scratch_shapes=[
            pltpu.VMEM((flat, chan), F32),
            pltpu.VMEM((flat, chan), BF16),
            pltpu.VMEM((flat, chan), BF16),
            pltpu.VMEM((flat, chan), BF16),
            pltpu.VMEM((flat, 4 * hid), F32),
            pltpu.VMEM((flat, 4 * hid), F32),
            pltpu.VMEM((flat, 4 * hid), F32),
            pltpu.VMEM((2, 4, 4, hid, chan), BF16),
        ],
        compiler_params=pltpu.CompilerParams(vmem_limit_bytes=40 * 1024 * 1024),
        name="both_updates",
    )(
        packed, packed_a, packed_e, half_b, half_f, w_e,
        chain_ids, chain_ids[:, None], pair_embed, in_gain, in_bias, gate_weight, out_gain, out_bias, out_weight,
    )


def layer_norm(values, gain, bias):
    mean = jnp.mean(values, axis=-1, keepdims=True)
    centered = values - mean
    var = jnp.mean(centered * centered, axis=-1, keepdims=True)
    return centered * lax.rsqrt(var + EPS) * gain + bias


def gated(normed, weights, maskf, form):
    proj = jnp.einsum(form, normed, weights, preferred_element_type=jnp.float32)
    return (jax.nn.sigmoid(proj[0]) * proj[1] * maskf).astype(jnp.bfloat16)


def outgoing(normed, weights, maskf):
    left = gated(normed, weights[0:2], maskf, "rnc,qch->qhrn")
    right = gated(normed, weights[2:4], maskf, "rnc,qch->qhrn")
    return jnp.einsum(
        "hik,hjk->hij",
        left,
        lax.all_gather(right, "row", axis=1, tiled=True),
        preferred_element_type=jnp.float32,
    ).astype(jnp.bfloat16)


def incoming(normed, weights, maskf):
    right = gated(normed, weights[2:4], maskf, "rnc,qch->qhrn")
    left = gated(normed, weights[0:2], maskf, "rnc,qch->qhrn")
    summed = jnp.transpose(
        lax.psum_scatter(
            jnp.einsum("hki,hkj->ihj", left, right, preferred_element_type=jnp.float32),
            "row",
            scatter_dimension=0,
            tiled=True,
        ),
        (1, 0, 2),
    )
    return summed.astype(jnp.bfloat16)


def finish(mixed, layer, out_gain, out_bias, out_weight):
    hid_full = out_weight.shape[1]
    whole = lax.all_gather(mixed, "ch", axis=0, tiled=True)
    values = whole.astype(jnp.float32)
    mean = jnp.sum(values, axis=0) / hid_full
    meansq = jnp.sum(values * values, axis=0) / hid_full
    gain = out_gain[layer]
    bias = out_bias[layer]
    weight = out_weight[layer]
    scale = lax.rsqrt(meansq - mean * mean + EPS)
    hidden = ((values - mean) * scale * gain[:, None, None] + bias[:, None, None]).astype(
        jnp.bfloat16
    )
    update = jnp.einsum("hrn,hc->rnc", hidden, weight, preferred_element_type=jnp.float32)
    return update


def fits(pair_shape, weight_shape):
    rows, n, chan = pair_shape
    hid = weight_shape[3]
    return (
        lax.axis_size("row") == 4
        and lax.axis_size("ch") == 4
        and rows * 4 == n
        and rows <= MASK_ROWS
        and rows % 2 == 0
        and n % 8 == 0
        and n <= chan
        and hid % 16 == 0
        and hid * 4 == chan
        and chan % 128 == 0
        and n * n * chan * 4 * 6 <= 16 * 1024 * 1024
    )


def per_device(
    pair,
    chain_ids,
    mask,
    pair_embed,
    in_gain,
    in_bias,
    proj_weight,
    gate_weight,
    out_gain,
    out_bias,
    out_weight,
):
    rows = pair.shape[0]
    if fits(pair.shape, proj_weight.shape):
        return in_one_phase(
            pair, chain_ids, mask, pair_embed, in_gain, in_bias, proj_weight, gate_weight, out_gain, out_bias, out_weight
        )
    start_row = lax.axis_index("row") * rows
    own_chain = lax.dynamic_slice_in_dim(chain_ids, start_row, rows, 0)
    same = (own_chain[:, None] == chain_ids[None, :])[:, :, None]
    current = pair.astype(jnp.float32) + jnp.where(same, pair_embed[1], pair_embed[0])
    maskf = mask.astype(jnp.float32)
    result = pair
    for layer in range(2):
        normed = layer_norm(current, in_gain[layer], in_bias[layer]).astype(jnp.bfloat16)
        weights = proj_weight[layer]
        if layer == 0:
            mixed = outgoing(normed, weights, maskf)
        else:
            mixed = incoming(normed, weights, maskf)
        update = finish(mixed, layer, out_gain, out_bias, out_weight)
        gate = jax.nn.sigmoid(
            jnp.dot(normed, gate_weight[layer], preferred_element_type=jnp.float32)
        )
        result = lax.optimization_barrier((current + gate * update).astype(jnp.bfloat16))
        current = result.astype(jnp.float32)
    return result


def solution(mesh):
    placed = (
        P(("grp", "row"), None, None),
        P("grp"),
        P(("grp", "row"), None),
        P(),
        P(),
        P(),
        P(None, None, None, "ch"),
        P(),
        P(),
        P(),
        P(),
    )
    return jax.shard_map(
        per_device,
        mesh=mesh,
        in_specs=placed,
        out_specs=P(("grp", "row"), None, None),
        check_vma=False,
    )
```

```python
import functools

import jax
import jax.numpy as jnp
from jax import lax
from jax.experimental import pallas as pl
from jax.experimental.pallas import tpu as pltpu
from jax.sharding import PartitionSpec as P

EPS = 1e-05
F32 = jnp.float32
BF16 = jnp.bfloat16
MASK_ROWS = 16


def nt_dot(a, b):
    return lax.dot_general(a, b, (((1,), (1,)), ((), ())), preferred_element_type=F32)


def nn_dot(a, b):
    return lax.dot_general(a, b, (((1,), (0,)), ((), ())), preferred_element_type=F32)


def half_sigmoid(half):
    return 0.5 * jnp.tanh(half) + 0.5


def normalize(values, gain, bias):
    mean = jnp.mean(values, axis=-1, keepdims=True)
    centered = values - mean
    var = jnp.mean(centered * centered, axis=-1, keepdims=True)
    return (centered * lax.rsqrt(var + EPS) * gain + bias).astype(BF16)


def pieces(rows, most):
    out, first = [], 0
    while first < rows:
        count = min(most, rows - first)
        out.append((first, count))
        first += count
    return out


def spread_masks(mask, rows, n, chan):
    spread = (
        lax.broadcasted_iota(jnp.int32, (rows, rows * chan), 1) // chan
        == lax.broadcasted_iota(jnp.int32, (rows, rows * chan), 0)
    ).astype(BF16)
    return lax.dot_general(mask.astype(BF16), spread, (((0,), (0,)), ((), ())), preferred_element_type=F32)


def lift(pair_rows, masks, chains, chain_s, embed, gain, bias, position, first, count):
    other, same = embed[0:1, :], embed[1:2, :]
    chan = chains.shape[1]
    z = jnp.concatenate(
        [jnp.where(chains == chain_s[position + i], same, other) for i in range(first, first + count)], axis=0
    ) + pair_rows.astype(F32)
    spread = jnp.concatenate([masks[:, i * chan : (i + 1) * chan] for i in range(first, first + count)], axis=0)
    return z, normalize(z, gain, bias), spread


def gated_side(zm, weights, u, side, chan):
    base = (u * 4 + side * 2) * chan
    both = nt_dot(zm, weights[base : base + 2 * chan, :])
    return (jnp.tanh(both[:, :chan]) + 1.0) * both[:, chan:]


def pack_kernel(n, rows, half, pair, mask, halved):
    core = lax.rem(lax.axis_index("ch"), 2)
    chan = pair.shape[1]
    masks = jnp.concatenate([mask[...].astype(F32), jnp.zeros((rows, chan - n), F32)], axis=1)
    masks = jnp.concatenate([masks, jnp.zeros((MASK_ROWS - rows, chan), F32)], axis=0).astype(BF16)
    start = pl.multiple_of(core * (rows - half) * n, 16)
    halved[0 : half * n, :] = pair[pl.ds(start, half * n), :]
    halved[half * n : half * n + MASK_ROWS, :] = masks


def weights_kernel(w_o, w_e, w_a, w_f, weights):
    c = lax.axis_index("ch")
    hid = w_o.shape[0] // 8
    for at, ref in enumerate((w_o, w_e, w_a, w_f)):
        for q in range(8):
            first = pl.multiple_of(q * 4 * hid + (c ^ at) * hid, 16)
            weights[pl.ds(first, hid), :] = ref[q * hid : (q + 1) * hid, :] * jnp.asarray(0.5, BF16)


def block_kernel(
    n, rows, which,
    pair, mask, weights, chain_s, chain_v, embed, in_gain, in_bias, gate_w,
    z_ref, g_ref, m_ref, left_ref, right_ref,
):
    r = lax.axis_index("row")
    core = lax.rem(lax.axis_index("ch"), 2)
    position = (r ^ which(core)) * rows
    chan = pair.shape[1]
    chains = jnp.broadcast_to(chain_v[...], (n, chan))
    masks = spread_masks(mask[...].astype(F32), rows, n, chan)
    for first, count in pieces(rows, 8):
        at = pl.ds(first * n, count * n)
        z, zn, spread = lift(
            pair[at, :], masks, chains, chain_s, embed, in_gain[0:1, :], in_bias[0:1, :], position, first, count
        )
        zm = zn * spread.astype(BF16)
        z_ref[at, :] = z
        m_ref[at, :] = spread
        g_ref[at, :] = jax.nn.sigmoid(nn_dot(zn, gate_w[0]))
        left_ref[at, :] = gated_side(zm, weights, 0, 0, chan)
        right_ref[at, :] = gated_side(zm, weights, 0, 1, chan)


def tiles_of(n, count, left_at, left_ref, left_step, steps, right_ref, right_at, width, right_step):
    def body(k, accs):
        right = right_ref[pl.ds(pl.multiple_of(right_at + k * right_step, 8), width), :]
        return tuple(acc + left_ref[pl.ds(left_at(i) + k * left_step, 1), :] * right for i, acc in enumerate(accs))

    chan = left_ref.shape[1]
    zeros = tuple(jnp.zeros((width, chan), F32) for _ in range(count))
    return lax.fori_loop(0, steps, body, zeros, unroll=min(8, steps))


def early_kernel(
    n, rows, early,
    z_o, z_a, z_e, g_o, g_a, g_e, m_o, m_a, m_e, left_o, left_a, left_e, right_o, right_a, right_e,
    x_ref, right_ref, z_ref, g_ref, m_ref, left_ref,
):
    core = lax.rem(lax.axis_index("ch"), 2)
    block, mid = rows * n, rows // 2 * n

    @pl.when(core == 0)
    def _():
        for out, o, a in ((z_ref, z_o, z_a), (g_ref, g_o, g_a), (m_ref, m_o, m_a), (left_ref, left_o, left_a)):
            out[0:block, :] = o[...]
            out[block : block + mid, :] = a[0:mid, :]

    @pl.when(core == 1)
    def _():
        for out, a, e in ((z_ref, z_a, z_e), (g_ref, g_a, g_e), (m_ref, m_a, m_e), (left_ref, left_a, left_e)):
            out[0:block, :] = a[...]
            out[block : block + mid, :] = e[mid:block, :]

    for j in range(rows):
        rows_of_j = slice(j * n, (j + 1) * n)
        right_ref[pl.ds(j, n, stride=n), :] = right_o[rows_of_j, :]
        right_ref[pl.ds(rows * (1 + core) + j, n, stride=n), :] = right_a[rows_of_j, :]
        right_ref[pl.ds(rows * (2 - core) + j, n, stride=n), :] = right_e[rows_of_j, :]

    group = rows // 2

    def some(t, _):
        first = t * group * n
        accs = tiles_of(n, group, lambda i: first + i * n, left_ref, 1, n, right_ref, 0, early, n)
        for i, acc in enumerate(accs):
            x_ref[pl.ds(pl.multiple_of(first + i * n, 8), early), :] = acc
        return 0

    lax.fori_loop(0, 3, some, 0)


def late_kernel(
    n, rows, half, early,
    half_b, half_f, weights, chain_s, chain_v, embed, in_gain, in_bias, gate_w, out_gain, out_bias, out_w,
    x_in, right_in, z_in, g_in, m_in, left_in,
    z1_ref, own_ref, m_ref,
    x_ref, late_ref, left_ref, z_ref, g_ref, zn_ref, mf_ref, zf_ref,
):
    r = lax.axis_index("row")
    core = lax.rem(lax.axis_index("ch"), 2)
    even = core == 0
    block, mid = rows * n, rows // 2 * n
    chan = half_b.shape[1]
    rest = rows - half
    late = n - early
    chains = jnp.broadcast_to(chain_v[...], (n, chan))
    masks = spread_masks(half_b[half * n : half * n + MASK_ROWS, 0:n][0:rows], rows, n, chan)
    skip = (half - rest) * n

    first_late = 3 * rows - early
    for t in range(first_late):
        late_ref[pl.ds(t, n, stride=late), :] = right_in[pl.ds(early + t, n, stride=n), :]
    for first, count in ((0, half), (half, rest)):
        size = count * n
        if first == 0:
            pair_rows = jnp.where(even, half_b[0:size, :], half_f[0:size, :])
        else:
            pair_rows = jnp.where(even, half_f[skip : skip + size, :], half_b[skip : skip + size, :])
        z, zn, spread = lift(
            pair_rows, masks, chains, chain_s, embed, in_gain[0:1, :], in_bias[0:1, :], (r ^ 3) * rows, first, count
        )
        zm = zn * spread.astype(BF16)
        right = gated_side(zm, weights, 0, 1, chan)
        for j in range(count):
            late_ref[pl.ds(first_late + first + j, n, stride=late), :] = right[j * n : (j + 1) * n]
        at = pl.ds(first * n, size)
        zf_ref[at, :] = z
        mf_ref[at, :] = spread
        zn_ref[at, :] = zn.astype(F32)

    own = pl.ds(pl.multiple_of(core * mid, 8), mid)
    tail = pl.ds(block + mid, mid)
    zn = zn_ref[own, :].astype(BF16)
    spread = mf_ref[own, :]
    left_ref[tail, :] = gated_side(zn * spread.astype(BF16), weights, 0, 0, chan)
    z_ref[tail, :] = zf_ref[own, :]
    g_ref[tail, :] = jax.nn.sigmoid(nn_dot(zn, gate_w[0]))
    m_ref[tail, :] = spread
    head = pl.ds(0, block + mid)
    left_ref[head, :] = left_in[...]
    z_ref[head, :] = z_in[...]
    g_ref[head, :] = g_in[...]
    m_ref[head, :] = m_in[...]

    group = rows // 2
    x_ref[head, :] = x_in[...]
    for i, acc in enumerate(
        tiles_of(n, group, lambda i: block + mid + i * n, left_ref, 1, n, right_in, 0, early, n)
    ):
        x_ref[pl.ds(block + mid + i * n, early), :] = acc
    for t in range(2):
        for i, acc in enumerate(
            tiles_of(n, rows, lambda i: t * block + i * n, left_ref, 1, n, late_ref, 0, late, late)
        ):
            x_ref[pl.ds(t * block + i * n + early, late), :] = acc

    def ordered(first, count):
        out = []
        for i in range(first, first + count):
            for b in range(4):
                out.append(x_ref[pl.ds(i * n + (r ^ b) * rows, rows), :])
        return jnp.concatenate(out, axis=0)

    for first, count in pieces(2 * rows, 8):
        at = pl.ds(first * n, count * n)
        update = hidden_update(ordered(first, count), out_gain[0:1, :], out_bias[0:1, :], out_w[0])
        z1 = (z_ref[at, :] + g_ref[at, :] * update).astype(BF16)
        z1_ref[at, :] = z1
        own_count = max(0, min(count, rows - first))
        if own_count:
            own_ref[pl.ds(first * n, own_count * n), :] = z1[: own_count * n]


def hidden_update(x, gain, bias, weight):
    mean = jnp.mean(x, axis=-1, keepdims=True)
    meansq = jnp.mean(x * x, axis=-1, keepdims=True)
    scale = lax.rsqrt(meansq - mean * mean + EPS)
    return nn_dot(((x - mean) * scale * gain + bias).astype(BF16), weight)


def incoming_kernel(n, rows, z1, masks, weights, in_gain, in_bias, part, left_ref, right_ref, sums_ref):
    r = lax.axis_index("row")
    chan = z1.shape[1]
    for first, count in pieces(2 * rows, 8):
        at = pl.ds(first * n, count * n)
        zn = normalize(z1[at, :].astype(F32), in_gain[1:2, :], in_bias[1:2, :])
        zm = zn * masks[at, :].astype(BF16)
        left_ref[at, :] = gated_side(zm, weights, 1, 0, chan)
        right_ref[at, :] = gated_side(zm, weights, 1, 1, chan)
    group = rows // 2
    wide = (n // 8 + 1) // 2 * 8
    for t in range(2):
        start = r * rows + t * group
        sums = [
            tiles_of(n, group, lambda i: start + i, left_ref, n, 2 * rows, right_ref, at, width, n)
            for at, width in ((0, wide), (wide, n - wide))
        ]
        for i in range(group):
            for (at, width), accs in zip(((0, wide), (wide, n - wide)), sums):
                left = (t * group + i) * n + at
                sums_ref[left : left + width, :] = accs[i]
    part[...] = sums_ref[...].astype(BF16)


def gate_kernel(own, received, in_gain, in_bias, gate_w, z_ref, g_ref):
    even = lax.rem(lax.axis_index("ch"), 2) == 0
    z = jnp.where(even, own[...], received[...]).astype(F32)
    z_ref[...] = z
    zn = normalize(z, in_gain[1:2, :], in_bias[1:2, :])
    g_ref[...] = jax.nn.sigmoid(nn_dot(zn, gate_w[1]))


def last_kernel(n, rows, part, received, z_ref, g_ref, out_gain, out_bias, out_w, result):
    for first, count in pieces(rows, 8):
        at = pl.ds(first * n, count * n)
        x = part[at, :].astype(F32) + received[at, :].astype(F32)
        update = hidden_update(x, out_gain[1:2, :], out_bias[1:2, :], out_w[1])
        out = (z_ref[at, :] + g_ref[at, :] * update).astype(BF16)
        for i in range(count):
            result[first + i] = out[i * n : (i + 1) * n]


def in_one_phase(
    pair, chain_ids, mask, pair_embed, in_gain, in_bias, proj_weight, gate_weight, out_gain, out_bias, out_weight
):
    rows, n, chan = pair.shape
    hid = proj_weight.shape[3]
    size = 8 * hid
    block, mid = rows * n, rows // 2 * n
    flat_pair = pair.reshape(block, chan)
    weights = jnp.transpose(proj_weight, (0, 1, 3, 2)).reshape(size, chan)
    half = (rows // 2 + 1) // 2 * 2
    early = 3 * rows // 8 * 8
    both = ("row", "ch")
    vmem = pl.BlockSpec(memory_space=pltpu.VMEM)
    smem = pl.BlockSpec(memory_space=pltpu.SMEM)

    def pairs_of(source):
        return [(source(r, c), r * 4 + c) for r in range(4) for c in range(4)]

    first = pairs_of(lambda r, c: (r ^ (1 + c % 2)) * 4 + (c ^ 2))
    second = pairs_of(lambda r, c: (r ^ 3) * 4 + c)
    cores = [(c, c ^ 1) for c in range(4)]

    def call(kernel, name, outs, ins, scalars=(), scratch=(), us=1.0):
        kept = [pltpu.with_memory_space_constraint(v, pltpu.VMEM) if id(v) in in_vmem else v for v in ins]
        specs = [smem if id(v) in scalars else vmem for v in ins]
        got = pl.pallas_call(
            kernel,
            out_shape=tuple(outs),
            in_specs=specs,
            out_specs=tuple(vmem for _ in outs),
            scratch_shapes=[pltpu.VMEM(s, F32) for s in scratch],
            compiler_params=pltpu.CompilerParams(vmem_limit_bytes=32 * 1024 * 1024),
            cost_estimate=pl.CostEstimate(flops=int(us * 1e9), bytes_accessed=0, transcendentals=0),
            name=name,
        )(*kept)
        for v in got:
            in_vmem[id(v)] = v
        return got

    in_vmem = {}
    f32 = lambda count: pltpu.VMEM((count, chan), F32)
    bf16 = lambda count: pltpu.VMEM((count, chan), BF16)
    chain_v = chain_ids[:, None]
    scalars = (id(chain_ids),)

    w_e = lax.ppermute(weights, "ch", cores)
    w_a, pair_a, mask_a = (lax.ppermute(v, both, first) for v in (weights, flat_pair, mask))
    (halved,) = call(
        functools.partial(pack_kernel, n, rows, half), "pack", [bf16(half * n + MASK_ROWS)], [flat_pair, mask]
    )
    half_b = lax.ppermute(halved, both, second)
    w_f, pair_e, mask_e = (lax.ppermute(v, "ch", cores) for v in (w_a, pair_a, mask_a))
    (w_all,) = call(weights_kernel, "weights", [bf16(4 * size)], [weights, w_e, w_a, w_f], us=0.1)
    half_f = lax.ppermute(half_b, "ch", cores)

    def one_block(name, which, pair_rows, mask_rows):
        return call(
            functools.partial(block_kernel, n, rows, which),
            name,
            [f32(block)] * 5,
            [pair_rows, mask_rows, w_all, chain_ids, chain_v, pair_embed, in_gain, in_bias, gate_weight],
            scalars,
        )

    at_o = one_block("own_block", lambda core: 0, flat_pair, mask)
    at_a = one_block("first_block", lambda core: 1 + core, pair_a, mask_a)
    at_e = one_block("second_block", lambda core: 2 - core, pair_e, mask_e)
    at_early = call(
        functools.partial(early_kernel, n, rows, early),
        "early",
        [f32(block + mid), f32(n * n)] + [f32(block + mid)] * 4,
        [v for three in zip(at_o, at_a, at_e) for v in three],
        us=2.0,
    )
    z1, own, masks = call(
        functools.partial(late_kernel, n, rows, half, early),
        "late",
        [bf16(2 * block), bf16(block), f32(2 * block)],
        [half_b, half_f, w_all, chain_ids, chain_v, pair_embed, in_gain, in_bias, gate_weight, out_gain, out_bias, out_weight]
        + list(at_early),
        scalars,
        [(2 * block, chan), (n * (n - early), chan)] + [(2 * block, chan)] * 3 + [(block, chan)] * 3,
        us=4.0,
    )
    own_n = lax.ppermute(own, "ch", cores)
    (part,) = call(
        functools.partial(incoming_kernel, n, rows),
        "incoming",
        [bf16(block)],
        [z1, masks, w_all, in_gain, in_bias],
        scratch=[(2 * block, chan)] * 2 + [(block, chan)],
        us=3.0,
    )
    part_n = lax.ppermute(part, "ch", cores)
    z1_own, gate = call(gate_kernel, "gate", [f32(block)] * 2, [own, own_n, in_gain, in_bias, gate_weight])
    (result,) = call(
        functools.partial(last_kernel, n, rows),
        "last",
        [jax.ShapeDtypeStruct((rows, n, chan), BF16)],
        [part, part_n, z1_own, gate, out_gain, out_bias, out_weight],
    )
    return result


def layer_norm(values, gain, bias):
    mean = jnp.mean(values, axis=-1, keepdims=True)
    centered = values - mean
    var = jnp.mean(centered * centered, axis=-1, keepdims=True)
    return centered * lax.rsqrt(var + EPS) * gain + bias


def gated(normed, weights, maskf, form):
    proj = jnp.einsum(form, normed, weights, preferred_element_type=jnp.float32)
    return (jax.nn.sigmoid(proj[0]) * proj[1] * maskf).astype(jnp.bfloat16)


def outgoing(normed, weights, maskf):
    left = gated(normed, weights[0:2], maskf, "rnc,qch->qhrn")
    right = gated(normed, weights[2:4], maskf, "rnc,qch->qhrn")
    return jnp.einsum(
        "hik,hjk->hij",
        left,
        lax.all_gather(right, "row", axis=1, tiled=True),
        preferred_element_type=jnp.float32,
    ).astype(jnp.bfloat16)


def incoming(normed, weights, maskf):
    right = gated(normed, weights[2:4], maskf, "rnc,qch->qhrn")
    left = gated(normed, weights[0:2], maskf, "rnc,qch->qhrn")
    summed = jnp.transpose(
        lax.psum_scatter(
            jnp.einsum("hki,hkj->ihj", left, right, preferred_element_type=jnp.float32),
            "row",
            scatter_dimension=0,
            tiled=True,
        ),
        (1, 0, 2),
    )
    return summed.astype(jnp.bfloat16)


def finish(mixed, layer, out_gain, out_bias, out_weight):
    hid_full = out_weight.shape[1]
    whole = lax.all_gather(mixed, "ch", axis=0, tiled=True)
    values = whole.astype(jnp.float32)
    mean = jnp.sum(values, axis=0) / hid_full
    meansq = jnp.sum(values * values, axis=0) / hid_full
    gain = out_gain[layer]
    bias = out_bias[layer]
    weight = out_weight[layer]
    scale = lax.rsqrt(meansq - mean * mean + EPS)
    hidden = ((values - mean) * scale * gain[:, None, None] + bias[:, None, None]).astype(
        jnp.bfloat16
    )
    update = jnp.einsum("hrn,hc->rnc", hidden, weight, preferred_element_type=jnp.float32)
    return update


def fits(pair_shape, weight_shape):
    rows, n, chan = pair_shape
    hid = weight_shape[3]
    return (
        lax.axis_size("row") == 4
        and lax.axis_size("ch") == 4
        and rows * 4 == n
        and rows <= MASK_ROWS
        and rows % 2 == 0
        and n % 8 == 0
        and n <= chan
        and hid % 16 == 0
        and hid * 4 == chan
        and chan % 128 == 0
        and n * n * chan * 4 * 6 <= 16 * 1024 * 1024
    )


def per_device(
    pair,
    chain_ids,
    mask,
    pair_embed,
    in_gain,
    in_bias,
    proj_weight,
    gate_weight,
    out_gain,
    out_bias,
    out_weight,
):
    rows = pair.shape[0]
    if fits(pair.shape, proj_weight.shape):
        return in_one_phase(
            pair, chain_ids, mask, pair_embed, in_gain, in_bias, proj_weight, gate_weight, out_gain, out_bias, out_weight
        )
    start_row = lax.axis_index("row") * rows
    own_chain = lax.dynamic_slice_in_dim(chain_ids, start_row, rows, 0)
    same = (own_chain[:, None] == chain_ids[None, :])[:, :, None]
    current = pair.astype(jnp.float32) + jnp.where(same, pair_embed[1], pair_embed[0])
    maskf = mask.astype(jnp.float32)
    result = pair
    for layer in range(2):
        normed = layer_norm(current, in_gain[layer], in_bias[layer]).astype(jnp.bfloat16)
        weights = proj_weight[layer]
        if layer == 0:
            mixed = outgoing(normed, weights, maskf)
        else:
            mixed = incoming(normed, weights, maskf)
        update = finish(mixed, layer, out_gain, out_bias, out_weight)
        gate = jax.nn.sigmoid(
            jnp.dot(normed, gate_weight[layer], preferred_element_type=jnp.float32)
        )
        result = lax.optimization_barrier((current + gate * update).astype(jnp.bfloat16))
        current = result.astype(jnp.float32)
    return result


def solution(mesh):
    placed = (
        P(("grp", "row"), None, None),
        P("grp"),
        P(("grp", "row"), None),
        P(),
        P(),
        P(),
        P(None, None, None, "ch"),
        P(),
        P(),
        P(),
        P(),
    )
    return jax.shard_map(
        per_device,
        mesh=mesh,
        in_specs=placed,
        out_specs=P(("grp", "row"), None, None),
        check_vma=False,
    )
```

```python
import functools

import jax
import jax.numpy as jnp
from jax import lax
from jax.experimental import pallas as pl
from jax.experimental.pallas import tpu as pltpu
from jax.sharding import PartitionSpec as P

EPS = 1e-05
F32 = jnp.float32
BF16 = jnp.bfloat16
MASK_ROWS = 16


def nt_dot(a, b):
    return lax.dot_general(a, b, (((1,), (1,)), ((), ())), preferred_element_type=F32)


def nn_dot(a, b):
    return lax.dot_general(a, b, (((1,), (0,)), ((), ())), preferred_element_type=F32)


def half_sigmoid(half):
    return 0.5 * jnp.tanh(half) + 0.5


def normalize(values, gain, bias):
    mean = jnp.mean(values, axis=-1, keepdims=True)
    centered = values - mean
    var = jnp.mean(centered * centered, axis=-1, keepdims=True)
    return (centered * lax.rsqrt(var + EPS) * gain + bias).astype(BF16)


def pieces(rows, most):
    out, first = [], 0
    while first < rows:
        count = min(most, rows - first)
        out.append((first, count))
        first += count
    return out


def spread_masks(mask, rows, n, chan):
    spread = (
        lax.broadcasted_iota(jnp.int32, (rows, rows * chan), 1) // chan
        == lax.broadcasted_iota(jnp.int32, (rows, rows * chan), 0)
    ).astype(BF16)
    return lax.dot_general(mask.astype(BF16), spread, (((0,), (0,)), ((), ())), preferred_element_type=F32)


def lift(pair_rows, masks, chains, embed, gain, bias, position, first, count):
    other, same = embed[0:1, :], embed[1:2, :]
    chan = chains.shape[1]
    z = jnp.concatenate(
        [
            jnp.where(chains[...] == chains[pl.ds(position + i, 1), :], same, other)
            for i in range(first, first + count)
        ],
        axis=0,
    ) + pair_rows.astype(F32)
    spread = jnp.concatenate([masks[:, i * chan : (i + 1) * chan] for i in range(first, first + count)], axis=0)
    return z, normalize(z, gain, bias), spread


def gated_side(zm, weights, u, side, chan):
    base = (u * 4 + side * 2) * chan
    both = nt_dot(zm, weights[base : base + 2 * chan, :])
    return (jnp.tanh(both[:, :chan]) + 1.0) * both[:, chan:]


def pack_kernel(n, rows, part, pair, mask, packed, halved, mask_v, sems):
    core = lax.rem(lax.axis_index("ch"), 2)
    block, chan = pair.shape
    start = pl.multiple_of(core * (block - part), 16)
    copies = [
        pltpu.make_async_copy(mask, mask_v, sems.at[0]),
        pltpu.make_async_copy(pair, packed.at[pl.ds(0, block)], sems.at[1]),
        pltpu.make_async_copy(pair.at[pl.ds(start, part)], halved.at[pl.ds(0, part)], sems.at[2]),
    ]
    for copy in copies:
        copy.start()
    copies[0].wait()
    masks = jnp.concatenate([mask_v[...].astype(F32), jnp.zeros((rows, chan - n), F32)], axis=1)
    masks = jnp.concatenate([masks, jnp.zeros((MASK_ROWS - rows, chan), F32)], axis=0).astype(BF16)
    packed[block : block + MASK_ROWS, :] = masks
    halved[part : part + MASK_ROWS, :] = masks
    copies[1].wait()
    copies[2].wait()


def constants_kernel(chain_row, *refs):
    count = (len(refs) - 3) // 2
    sources, outs = refs[:count], refs[count : 2 * count]
    chains, row, sems = refs[2 * count :]
    first = pltpu.make_async_copy(chain_row, row, sems.at[count])
    first.start()
    copies = [pltpu.make_async_copy(a, b, sems.at[i]) for i, (a, b) in enumerate(zip(sources, outs))]
    for copy in copies:
        copy.start()
    first.wait()
    ones = jnp.ones((1, chains.shape[1]), BF16)
    chains[...] = lax.dot_general(
        row[...].astype(F32).astype(BF16), ones, (((0,), (0,)), ((), ())), preferred_element_type=F32
    )
    for copy in copies:
        copy.wait()


def pass_kernel(value, after, out):
    out[...] = value[...]


def weights_kernel(w_o, w_e, w_a, w_f, weights):
    c = lax.axis_index("ch")
    hid = w_e.shape[0] // 8
    for at, ref in enumerate((w_o, w_e, w_a, w_f)):
        for q in range(8):
            first = pl.multiple_of(q * 4 * hid + (c ^ at) * hid, 16)
            weights[pl.ds(first, hid), :] = ref[q * hid : (q + 1) * hid, :] * jnp.asarray(0.5, BF16)


def lift_kernel(
    n, rows, which,
    packed, chains, embed, in_gain, in_bias, gate_w,
    z_ref, g_ref, m_ref, zm_ref,
):
    r = lax.axis_index("row")
    core = lax.rem(lax.axis_index("ch"), 2)
    position = (r ^ which(core)) * rows
    chan = packed.shape[1]
    masks_at = packed.shape[0] - MASK_ROWS
    masks = spread_masks(packed[masks_at : masks_at + MASK_ROWS, 0:n][0:rows], rows, n, chan)
    for first, count in pieces(rows, 8):
        at = pl.ds(first * n, count * n)
        z, zn, spread = lift(
            packed[at, :], masks, chains, embed, in_gain[0:1, :], in_bias[0:1, :], position, first, count
        )
        z_ref[at, :] = z
        m_ref[at, :] = spread
        g_ref[at, :] = jax.nn.sigmoid(nn_dot(zn, gate_w[0]))
        zm_ref[at, :] = zn * spread.astype(BF16)


def project_kernel(n, rows, zm_ref, weights, left_ref, right_ref):
    chan = zm_ref.shape[1]
    for first, count in pieces(rows, 8):
        at = pl.ds(first * n, count * n)
        zm = zm_ref[at, :]
        left_ref[at, :] = gated_side(zm, weights, 0, 0, chan)
        right_ref[at, :] = gated_side(zm, weights, 0, 1, chan)


def tiles_of(n, count, left_at, left_ref, left_step, steps, right_ref, right_at, width, right_step):
    def body(k, accs):
        right = right_ref[pl.ds(pl.multiple_of(right_at + k * right_step, 8), width), :]
        return tuple(acc + left_ref[pl.ds(left_at(i) + k * left_step, 1), :] * right for i, acc in enumerate(accs))

    chan = left_ref.shape[1]
    zeros = tuple(jnp.zeros((width, chan), F32) for _ in range(count))
    return lax.fori_loop(0, steps, body, zeros, unroll=min(8, steps))


def early_kernel(
    n, rows, early,
    z_o, z_a, z_e, g_o, g_a, g_e, m_o, m_a, m_e, left_o, left_a, left_e, right_o, right_a, right_e,
    x_ref, right_ref, z_ref, g_ref, m_ref, left_ref,
):
    core = lax.rem(lax.axis_index("ch"), 2)
    block, mid = rows * n, rows // 2 * n

    @pl.when(core == 0)
    def _():
        for out, o, a in ((z_ref, z_o, z_a), (g_ref, g_o, g_a), (m_ref, m_o, m_a), (left_ref, left_o, left_a)):
            out[0:block, :] = o[...]
            out[block : block + mid, :] = a[0:mid, :]

    @pl.when(core == 1)
    def _():
        for out, a, e in ((z_ref, z_a, z_e), (g_ref, g_a, g_e), (m_ref, m_a, m_e), (left_ref, left_a, left_e)):
            out[0:block, :] = a[...]
            out[block : block + mid, :] = e[mid:block, :]

    for j in range(rows):
        rows_of_j = slice(j * n, (j + 1) * n)
        right_ref[pl.ds(j, n, stride=n), :] = right_o[rows_of_j, :]
        right_ref[pl.ds(rows * (1 + core) + j, n, stride=n), :] = right_a[rows_of_j, :]
        right_ref[pl.ds(rows * (2 - core) + j, n, stride=n), :] = right_e[rows_of_j, :]

    group = rows // 2

    def some(t, _):
        first = t * group * n
        accs = tiles_of(n, group, lambda i: first + i * n, left_ref, 1, n, right_ref, 0, early, n)
        for i, acc in enumerate(accs):
            x_ref[pl.ds(pl.multiple_of(first + i * n, 8), early), :] = acc
        return 0

    lax.fori_loop(0, 3, some, 0)


def late_kernel(
    n, rows, part, early,
    half_b, half_f, weights, chains, embed, in_gain, in_bias, gate_w, out_gain, out_bias, out_w,
    x_in, right_in, z_in, g_in, m_in, left_in,
    z1_ref, own_ref, m_ref,
    x_ref, late_ref, left_ref, z_ref, g_ref, zn_ref, mf_ref, zf_ref,
):
    r = lax.axis_index("row")
    core = lax.rem(lax.axis_index("ch"), 2)
    even = core == 0
    block, mid = rows * n, rows // 2 * n
    chan = half_b.shape[1]
    late = n - early
    masks = spread_masks(half_b[part : part + MASK_ROWS, 0:n][0:rows], rows, n, chan)
    skip = 2 * part - block
    pair_rows = jnp.concatenate(
        [
            jnp.where(even, half_b[0:part, :], half_f[0:part, :]),
            jnp.where(even, half_f[skip:part, :], half_b[skip:part, :]),
        ],
        axis=0,
    )

    first_late = 3 * rows - early
    for t in range(first_late):
        late_ref[pl.ds(t, n, stride=late), :] = right_in[pl.ds(early + t, n, stride=n), :]
    for first, count in pieces(rows, 8):
        size = count * n
        z, zn, spread = lift(
            pair_rows[first * n : first * n + size], masks, chains, embed, in_gain[0:1, :], in_bias[0:1, :],
            (r ^ 3) * rows, first, count,
        )
        zm = zn * spread.astype(BF16)
        right = gated_side(zm, weights, 0, 1, chan)
        for j in range(count):
            late_ref[pl.ds(first_late + first + j, n, stride=late), :] = right[j * n : (j + 1) * n]
        at = pl.ds(first * n, size)
        zf_ref[at, :] = z
        mf_ref[at, :] = spread
        zn_ref[at, :] = zn.astype(F32)

    own = pl.ds(pl.multiple_of(core * mid, 8), mid)
    tail = pl.ds(block + mid, mid)
    zn = zn_ref[own, :].astype(BF16)
    spread = mf_ref[own, :]
    left_ref[tail, :] = gated_side(zn * spread.astype(BF16), weights, 0, 0, chan)
    z_ref[tail, :] = zf_ref[own, :]
    g_ref[tail, :] = jax.nn.sigmoid(nn_dot(zn, gate_w[0]))
    m_ref[tail, :] = spread
    head = pl.ds(0, block + mid)
    left_ref[head, :] = left_in[...]
    z_ref[head, :] = z_in[...]
    g_ref[head, :] = g_in[...]
    m_ref[head, :] = m_in[...]

    group = rows // 2
    x_ref[head, :] = x_in[...]
    for i, acc in enumerate(
        tiles_of(n, group, lambda i: block + mid + i * n, left_ref, 1, n, right_in, 0, early, n)
    ):
        x_ref[pl.ds(block + mid + i * n, early), :] = acc
    for t in range(2):
        for i, acc in enumerate(
            tiles_of(n, rows, lambda i: t * block + i * n, left_ref, 1, n, late_ref, 0, late, late)
        ):
            x_ref[pl.ds(t * block + i * n + early, late), :] = acc

    def ordered(first, count):
        out = []
        for i in range(first, first + count):
            for b in range(4):
                out.append(x_ref[pl.ds(i * n + (r ^ b) * rows, rows), :])
        return jnp.concatenate(out, axis=0)

    for first, count in pieces(2 * rows, 8):
        at = pl.ds(first * n, count * n)
        update = hidden_update(ordered(first, count), out_gain[0:1, :], out_bias[0:1, :], out_w[0])
        z1 = (z_ref[at, :] + g_ref[at, :] * update).astype(BF16)
        z1_ref[at, :] = z1
        own_count = max(0, min(count, rows - first))
        if own_count:
            own_ref[pl.ds(first * n, own_count * n), :] = z1[: own_count * n]


def hidden_update(x, gain, bias, weight):
    mean = jnp.mean(x, axis=-1, keepdims=True)
    meansq = jnp.mean(x * x, axis=-1, keepdims=True)
    scale = lax.rsqrt(meansq - mean * mean + EPS)
    return nn_dot(((x - mean) * scale * gain + bias).astype(BF16), weight)


def incoming_kernel(n, rows, z1, masks, weights, in_gain, in_bias, part, left_ref, right_ref, sums_ref):
    r = lax.axis_index("row")
    chan = z1.shape[1]
    for first, count in pieces(2 * rows, 8):
        at = pl.ds(first * n, count * n)
        zn = normalize(z1[at, :].astype(F32), in_gain[1:2, :], in_bias[1:2, :])
        zm = zn * masks[at, :].astype(BF16)
        left_ref[at, :] = gated_side(zm, weights, 1, 0, chan)
        right_ref[at, :] = gated_side(zm, weights, 1, 1, chan)
    group = rows // 2
    wide = (n // 8 + 1) // 2 * 8
    for t in range(2):
        start = r * rows + t * group
        sums = [
            tiles_of(n, group, lambda i: start + i, left_ref, n, 2 * rows, right_ref, at, width, n)
            for at, width in ((0, wide), (wide, n - wide))
        ]
        for i in range(group):
            for (at, width), accs in zip(((0, wide), (wide, n - wide)), sums):
                left = (t * group + i) * n + at
                sums_ref[left : left + width, :] = accs[i]
    part[...] = sums_ref[...].astype(BF16)


def gate_kernel(own, received, in_gain, in_bias, gate_w, z_ref, g_ref):
    even = lax.rem(lax.axis_index("ch"), 2) == 0
    z = jnp.where(even, own[...], received[...]).astype(F32)
    z_ref[...] = z
    zn = normalize(z, in_gain[1:2, :], in_bias[1:2, :])
    g_ref[...] = jax.nn.sigmoid(nn_dot(zn, gate_w[1]))


def last_kernel(n, rows, part, received, z_ref, g_ref, out_gain, out_bias, out_w, result):
    for first, count in pieces(rows, 8):
        at = pl.ds(first * n, count * n)
        x = part[at, :].astype(F32) + received[at, :].astype(F32)
        update = hidden_update(x, out_gain[1:2, :], out_bias[1:2, :], out_w[1])
        out = (z_ref[at, :] + g_ref[at, :] * update).astype(BF16)
        for i in range(count):
            result[first + i] = out[i * n : (i + 1) * n]


def in_one_phase(
    pair, chain_ids, mask, pair_embed, in_gain, in_bias, proj_weight, gate_weight, out_gain, out_bias, out_weight
):
    rows, n, chan = pair.shape
    hid = proj_weight.shape[3]
    size = 8 * hid
    block, mid = rows * n, rows // 2 * n
    flat_pair = pair.reshape(block, chan)
    weights = jnp.transpose(proj_weight, (0, 1, 3, 2)).reshape(size, chan)
    part = (block // 2 + 15) // 16 * 16
    early = 3 * rows // 8 * 8
    both = ("row", "ch")
    vmem = pl.BlockSpec(memory_space=pltpu.VMEM)

    def pairs_of(source):
        return [(source(r, c), r * 4 + c) for r in range(4) for c in range(4)]

    first = pairs_of(lambda r, c: (r ^ (1 + c % 2)) * 4 + c)
    second = pairs_of(lambda r, c: (r ^ 3) * 4 + c)
    cores = [(c, c ^ 1) for c in range(4)]
    chips = [(c, c ^ 2) for c in range(4)]

    def call(kernel, name, outs, ins, scratch=(), us=1.0):
        kept = [pltpu.with_memory_space_constraint(v, pltpu.VMEM) if id(v) in in_vmem else v for v in ins]
        got = pl.pallas_call(
            kernel,
            out_shape=tuple(outs),
            in_specs=[vmem] * len(ins),
            out_specs=tuple(vmem for _ in outs),
            scratch_shapes=[pltpu.VMEM(s, F32) for s in scratch],
            compiler_params=pltpu.CompilerParams(vmem_limit_bytes=32 * 1024 * 1024),
            cost_estimate=pl.CostEstimate(flops=int(us * 1e9), bytes_accessed=0, transcendentals=0),
            name=name,
        )(*kept)
        for v in got:
            in_vmem[id(v)] = v
        return got

    in_vmem = {}
    f32 = lambda count: pltpu.VMEM((count, chan), F32)
    bf16 = lambda count: pltpu.VMEM((count, chan), BF16)

    packed, halved = pl.pallas_call(
        functools.partial(pack_kernel, n, rows, part),
        out_shape=(bf16(block + MASK_ROWS), bf16(part + MASK_ROWS)),
        in_specs=[pl.BlockSpec(memory_space=pl.ANY)] * 2,
        out_specs=(vmem, vmem),
        scratch_shapes=[pltpu.VMEM((rows, n), jnp.int32), pltpu.SemaphoreType.DMA((3,))],
        name="pack",
    )(*(pltpu.with_memory_space_constraint(v, pltpu.HBM) for v in (flat_pair, mask)))
    sources = (weights, pair_embed, in_gain, in_bias, gate_weight, out_gain, out_bias, out_weight)
    constants = pl.pallas_call(
        constants_kernel,
        out_shape=tuple(pltpu.VMEM(v.shape, v.dtype) for v in sources) + (pltpu.VMEM((n, chan), F32),),
        in_specs=[pl.BlockSpec(memory_space=pl.ANY)] * (1 + len(sources)),
        out_specs=tuple(vmem for _ in range(1 + len(sources))),
        scratch_shapes=[pltpu.VMEM((1, n), jnp.int32), pltpu.SemaphoreType.DMA((1 + len(sources),))],
        name="constants",
    )(*(pltpu.with_memory_space_constraint(v, pltpu.HBM) for v in (chain_ids.reshape(1, n),) + sources))
    in_vmem.update({id(v): v for v in (packed, halved) + tuple(constants)})
    w_own, pair_embed, in_gain, in_bias, gate_weight, out_gain, out_bias, out_weight, chains = constants
    packed_a = lax.ppermute(packed, both, first)
    half_b = lax.ppermute(halved, both, second)
    w_e = lax.ppermute(weights, "ch", cores)
    w_a = lax.ppermute(weights, "ch", chips)
    w_f = lax.ppermute(w_a, "ch", cores)
    packed_e = lax.ppermute(packed_a, "ch", cores)

    def one_block(name, which, source):
        return call(
            functools.partial(lift_kernel, n, rows, which),
            name,
            [f32(block)] * 3 + [bf16(block)],
            [source, chains, pair_embed, in_gain, in_bias, gate_weight],
            us=0.8,
        )

    at_o = one_block("lift_own", lambda core: 0, packed)
    at_a = one_block("lift_first", lambda core: 1 + core, packed_a)
    (w_all,) = call(weights_kernel, "weights", [bf16(4 * size)], [w_own, w_e, w_a, w_f], us=0.1)
    at_e = one_block("lift_second", lambda core: 2 - core, packed_e)

    def project(name, lifted):
        sides = call(functools.partial(project_kernel, n, rows), name, [f32(block)] * 2, [lifted[3], w_all], us=0.6)
        return list(lifted[:3]) + list(sides)

    at_o, at_a, at_e = (
        project(name, v) for name, v in (("project_own", at_o), ("project_first", at_a), ("project_second", at_e))
    )
    (half_b,) = call(pass_kernel, "pass_on", [bf16(part + MASK_ROWS)], [half_b, at_e[4]], us=0.1)
    half_f = lax.ppermute(half_b, "ch", cores)
    at_early = call(
        functools.partial(early_kernel, n, rows, early),
        "early",
        [f32(block + mid), f32(n * n)] + [f32(block + mid)] * 4,
        [v for three in zip(at_o, at_a, at_e) for v in three],
        us=2.0,
    )
    z1, own, masks = call(
        functools.partial(late_kernel, n, rows, part, early),
        "late",
        [bf16(2 * block), bf16(block), f32(2 * block)],
        [half_b, half_f, w_all, chains, pair_embed, in_gain, in_bias, gate_weight, out_gain, out_bias, out_weight]
        + list(at_early),
        [(2 * block, chan), (n * (n - early), chan)] + [(2 * block, chan)] * 3 + [(block, chan)] * 3,
        us=4.0,
    )
    own_n = lax.ppermute(own, "ch", cores)
    (part,) = call(
        functools.partial(incoming_kernel, n, rows),
        "incoming",
        [bf16(block)],
        [z1, masks, w_all, in_gain, in_bias],
        scratch=[(2 * block, chan)] * 2 + [(block, chan)],
        us=3.0,
    )
    part_n = lax.ppermute(part, "ch", cores)
    z1_own, gate = call(gate_kernel, "gate", [f32(block)] * 2, [own, own_n, in_gain, in_bias, gate_weight])
    (result,) = call(
        functools.partial(last_kernel, n, rows),
        "last",
        [jax.ShapeDtypeStruct((rows, n, chan), BF16)],
        [part, part_n, z1_own, gate, out_gain, out_bias, out_weight],
    )
    return result


def layer_norm(values, gain, bias):
    mean = jnp.mean(values, axis=-1, keepdims=True)
    centered = values - mean
    var = jnp.mean(centered * centered, axis=-1, keepdims=True)
    return centered * lax.rsqrt(var + EPS) * gain + bias


def gated(normed, weights, maskf, form):
    proj = jnp.einsum(form, normed, weights, preferred_element_type=jnp.float32)
    return (jax.nn.sigmoid(proj[0]) * proj[1] * maskf).astype(jnp.bfloat16)


def outgoing(normed, weights, maskf):
    left = gated(normed, weights[0:2], maskf, "rnc,qch->qhrn")
    right = gated(normed, weights[2:4], maskf, "rnc,qch->qhrn")
    return jnp.einsum(
        "hik,hjk->hij",
        left,
        lax.all_gather(right, "row", axis=1, tiled=True),
        preferred_element_type=jnp.float32,
    ).astype(jnp.bfloat16)


def incoming(normed, weights, maskf):
    right = gated(normed, weights[2:4], maskf, "rnc,qch->qhrn")
    left = gated(normed, weights[0:2], maskf, "rnc,qch->qhrn")
    summed = jnp.transpose(
        lax.psum_scatter(
            jnp.einsum("hki,hkj->ihj", left, right, preferred_element_type=jnp.float32),
            "row",
            scatter_dimension=0,
            tiled=True,
        ),
        (1, 0, 2),
    )
    return summed.astype(jnp.bfloat16)


def finish(mixed, layer, out_gain, out_bias, out_weight):
    hid_full = out_weight.shape[1]
    whole = lax.all_gather(mixed, "ch", axis=0, tiled=True)
    values = whole.astype(jnp.float32)
    mean = jnp.sum(values, axis=0) / hid_full
    meansq = jnp.sum(values * values, axis=0) / hid_full
    gain = out_gain[layer]
    bias = out_bias[layer]
    weight = out_weight[layer]
    scale = lax.rsqrt(meansq - mean * mean + EPS)
    hidden = ((values - mean) * scale * gain[:, None, None] + bias[:, None, None]).astype(
        jnp.bfloat16
    )
    update = jnp.einsum("hrn,hc->rnc", hidden, weight, preferred_element_type=jnp.float32)
    return update


def fits(pair_shape, weight_shape):
    rows, n, chan = pair_shape
    hid = weight_shape[3]
    return (
        lax.axis_size("row") == 4
        and lax.axis_size("ch") == 4
        and rows * 4 == n
        and rows <= MASK_ROWS
        and rows % 2 == 0
        and n % 8 == 0
        and n <= chan
        and hid % 16 == 0
        and hid * 4 == chan
        and chan % 128 == 0
        and n * n * chan * 4 * 6 <= 16 * 1024 * 1024
    )


def per_device(
    pair,
    chain_ids,
    mask,
    pair_embed,
    in_gain,
    in_bias,
    proj_weight,
    gate_weight,
    out_gain,
    out_bias,
    out_weight,
):
    rows = pair.shape[0]
    if fits(pair.shape, proj_weight.shape):
        return in_one_phase(
            pair, chain_ids, mask, pair_embed, in_gain, in_bias, proj_weight, gate_weight, out_gain, out_bias, out_weight
        )
    start_row = lax.axis_index("row") * rows
    own_chain = lax.dynamic_slice_in_dim(chain_ids, start_row, rows, 0)
    same = (own_chain[:, None] == chain_ids[None, :])[:, :, None]
    current = pair.astype(jnp.float32) + jnp.where(same, pair_embed[1], pair_embed[0])
    maskf = mask.astype(jnp.float32)
    result = pair
    for layer in range(2):
        normed = layer_norm(current, in_gain[layer], in_bias[layer]).astype(jnp.bfloat16)
        weights = proj_weight[layer]
        if layer == 0:
            mixed = outgoing(normed, weights, maskf)
        else:
            mixed = incoming(normed, weights, maskf)
        update = finish(mixed, layer, out_gain, out_bias, out_weight)
        gate = jax.nn.sigmoid(
            jnp.dot(normed, gate_weight[layer], preferred_element_type=jnp.float32)
        )
        result = lax.optimization_barrier((current + gate * update).astype(jnp.bfloat16))
        current = result.astype(jnp.float32)
    return result


def solution(mesh):
    placed = (
        P(("grp", "row"), None, None),
        P("grp"),
        P(("grp", "row"), None),
        P(),
        P(),
        P(),
        P(None, None, None, "ch"),
        P(),
        P(),
        P(),
        P(),
    )
    return jax.shard_map(
        per_device,
        mesh=mesh,
        in_specs=placed,
        out_specs=P(("grp", "row"), None, None),
        check_vma=False,
    )
```

```python
import functools

import jax
import jax.numpy as jnp
from jax import lax
from jax.experimental import pallas as pl
from jax.experimental.pallas import tpu as pltpu
from jax.sharding import PartitionSpec as P

EPS = 1e-05
F32 = jnp.float32
BF16 = jnp.bfloat16
MASK_ROWS = 16


def nt_dot(a, b):
    return lax.dot_general(a, b, (((1,), (1,)), ((), ())), preferred_element_type=F32)


def nn_dot(a, b):
    return lax.dot_general(a, b, (((1,), (0,)), ((), ())), preferred_element_type=F32)


def half_sigmoid(half):
    return 0.5 * jnp.tanh(half) + 0.5


def normalize(values, gain, bias):
    mean = jnp.mean(values, axis=-1, keepdims=True)
    centered = values - mean
    var = jnp.mean(centered * centered, axis=-1, keepdims=True)
    return (centered * lax.rsqrt(var + EPS) * gain + bias).astype(BF16)


def pieces(rows, most):
    out, first = [], 0
    while first < rows:
        count = min(most, rows - first)
        out.append((first, count))
        first += count
    return out


def spread_masks(mask, rows, n, chan):
    spread = (
        lax.broadcasted_iota(jnp.int32, (rows, rows * chan), 1) // chan
        == lax.broadcasted_iota(jnp.int32, (rows, rows * chan), 0)
    ).astype(BF16)
    return lax.dot_general(mask.astype(BF16), spread, (((0,), (0,)), ((), ())), preferred_element_type=F32)


def lift(pair_rows, masks, chains, embed, gain, bias, position, first, count):
    other, same = embed[0:1, :], embed[1:2, :]
    chan = chains.shape[1]
    z = jnp.concatenate(
        [
            jnp.where(chains[...] == chains[pl.ds(position + i, 1), :], same, other)
            for i in range(first, first + count)
        ],
        axis=0,
    ) + pair_rows.astype(F32)
    spread = jnp.concatenate([masks[:, i * chan : (i + 1) * chan] for i in range(first, first + count)], axis=0)
    return z, normalize(z, gain, bias), spread


def gated_side(zm, weights, u, side, chan):
    base = (u * 4 + side * 2) * chan
    both = nt_dot(zm, weights[base : base + 2 * chan, :])
    return (jnp.tanh(both[:, :chan]) + 1.0) * both[:, chan:]


def pack_kernel(n, rows, pair, mask, packed, mask_v, sems):
    block, chan = pair.shape
    copies = [
        pltpu.make_async_copy(mask, mask_v, sems.at[0]),
        pltpu.make_async_copy(pair, packed.at[pl.ds(0, block)], sems.at[1]),
    ]
    for copy in copies:
        copy.start()
    copies[0].wait()
    wide = jnp.concatenate([mask_v[...].astype(F32), jnp.zeros((rows, chan - n), F32)], axis=1)
    packed[block : block + MASK_ROWS, :] = jnp.concatenate(
        [wide, jnp.zeros((MASK_ROWS - rows, chan), F32)], axis=0
    ).astype(BF16)
    copies[1].wait()


def constants_kernel(part, packed, chain_row, *refs):
    count = (len(refs) - 4) // 2
    sources, outs = refs[:count], refs[count : 2 * count]
    chains, halved, row, sems = refs[2 * count :]
    first = pltpu.make_async_copy(chain_row, row, sems.at[count])
    first.start()
    copies = [pltpu.make_async_copy(a, b, sems.at[i]) for i, (a, b) in enumerate(zip(sources, outs))]
    for copy in copies:
        copy.start()
    core = lax.rem(lax.axis_index("ch"), 2)
    block = packed.shape[0] - MASK_ROWS
    start = pl.multiple_of(core * (block - part), 16)
    halved[0:part, :] = packed[pl.ds(start, part), :]
    halved[part : part + MASK_ROWS, :] = packed[block : block + MASK_ROWS, :]
    first.wait()
    ones = jnp.ones((1, chains.shape[1]), BF16)
    chains[...] = lax.dot_general(
        row[...].astype(F32).astype(BF16), ones, (((0,), (0,)), ((), ())), preferred_element_type=F32
    )
    for copy in copies:
        copy.wait()


def pass_kernel(value, after, out):
    out[...] = value[...]


def weights_kernel(w_o, w_e, w_a, w_f, weights):
    c = lax.axis_index("ch")
    hid = w_e.shape[0] // 8
    for at, ref in enumerate((w_o, w_e, w_a, w_f)):
        for q in range(8):
            first = pl.multiple_of(q * 4 * hid + (c ^ at) * hid, 16)
            weights[pl.ds(first, hid), :] = ref[q * hid : (q + 1) * hid, :] * jnp.asarray(0.5, BF16)


def lift_kernel(
    n, rows, which,
    packed, chains, embed, in_gain, in_bias, gate_w,
    z_ref, g_ref, m_ref, zm_ref,
):
    r = lax.axis_index("row")
    core = lax.rem(lax.axis_index("ch"), 2)
    position = (r ^ which(core)) * rows
    chan = packed.shape[1]
    masks_at = packed.shape[0] - MASK_ROWS
    masks = spread_masks(packed[masks_at : masks_at + MASK_ROWS, 0:n][0:rows], rows, n, chan)
    for first, count in pieces(rows, 8):
        at = pl.ds(first * n, count * n)
        z, zn, spread = lift(
            packed[at, :], masks, chains, embed, in_gain[0:1, :], in_bias[0:1, :], position, first, count
        )
        z_ref[at, :] = z
        m_ref[at, :] = spread
        g_ref[at, :] = jax.nn.sigmoid(nn_dot(zn, gate_w[0]))
        zm_ref[at, :] = zn * spread.astype(BF16)


def project_kernel(n, rows, zm_ref, weights, left_ref, right_ref):
    chan = zm_ref.shape[1]
    for first, count in pieces(rows, 8):
        at = pl.ds(first * n, count * n)
        zm = zm_ref[at, :]
        left_ref[at, :] = gated_side(zm, weights, 0, 0, chan)
        right_ref[at, :] = gated_side(zm, weights, 0, 1, chan)


def tiles_of(n, count, left_at, left_ref, left_step, steps, right_ref, right_at, width, right_step):
    def body(k, accs):
        right = right_ref[pl.ds(pl.multiple_of(right_at + k * right_step, 8), width), :]
        return tuple(acc + left_ref[pl.ds(left_at(i) + k * left_step, 1), :] * right for i, acc in enumerate(accs))

    chan = left_ref.shape[1]
    zeros = tuple(jnp.zeros((width, chan), F32) for _ in range(count))
    return lax.fori_loop(0, steps, body, zeros, unroll=min(8, steps))


def early_kernel(
    n, rows, early,
    z_o, z_a, z_e, g_o, g_a, g_e, m_o, m_a, m_e, left_o, left_a, left_e, right_o, right_a, right_e,
    x_ref, right_ref, z_ref, g_ref, m_ref, left_ref,
):
    core = lax.rem(lax.axis_index("ch"), 2)
    block, mid = rows * n, rows // 2 * n

    @pl.when(core == 0)
    def _():
        for out, o, a in ((z_ref, z_o, z_a), (g_ref, g_o, g_a), (m_ref, m_o, m_a), (left_ref, left_o, left_a)):
            out[0:block, :] = o[...]
            out[block : block + mid, :] = a[0:mid, :]

    @pl.when(core == 1)
    def _():
        for out, a, e in ((z_ref, z_a, z_e), (g_ref, g_a, g_e), (m_ref, m_a, m_e), (left_ref, left_a, left_e)):
            out[0:block, :] = a[...]
            out[block : block + mid, :] = e[mid:block, :]

    for j in range(rows):
        rows_of_j = slice(j * n, (j + 1) * n)
        right_ref[pl.ds(j, n, stride=n), :] = right_o[rows_of_j, :]
        right_ref[pl.ds(rows * (1 + core) + j, n, stride=n), :] = right_a[rows_of_j, :]
        right_ref[pl.ds(rows * (2 - core) + j, n, stride=n), :] = right_e[rows_of_j, :]

    group = rows // 2

    def some(t, _):
        first = t * group * n
        accs = tiles_of(n, group, lambda i: first + i * n, left_ref, 1, n, right_ref, 0, early, n)
        for i, acc in enumerate(accs):
            x_ref[pl.ds(pl.multiple_of(first + i * n, 8), early), :] = acc
        return 0

    lax.fori_loop(0, 3, some, 0)


def late_kernel(
    n, rows, part, early,
    half_b, half_f, weights, chains, embed, in_gain, in_bias, gate_w, out_gain, out_bias, out_w,
    x_in, right_in, z_in, g_in, m_in, left_in,
    z1_ref, own_ref, m_ref,
    x_ref, late_ref, left_ref, z_ref, g_ref, zn_ref, mf_ref, zf_ref,
):
    r = lax.axis_index("row")
    core = lax.rem(lax.axis_index("ch"), 2)
    even = core == 0
    block, mid = rows * n, rows // 2 * n
    chan = half_b.shape[1]
    late = n - early
    masks = spread_masks(half_b[part : part + MASK_ROWS, 0:n][0:rows], rows, n, chan)
    skip = 2 * part - block
    pair_rows = jnp.concatenate(
        [
            jnp.where(even, half_b[0:part, :], half_f[0:part, :]),
            jnp.where(even, half_f[skip:part, :], half_b[skip:part, :]),
        ],
        axis=0,
    )

    first_late = 3 * rows - early
    for t in range(first_late):
        late_ref[pl.ds(t, n, stride=late), :] = right_in[pl.ds(early + t, n, stride=n), :]
    for first, count in pieces(rows, 8):
        size = count * n
        z, zn, spread = lift(
            pair_rows[first * n : first * n + size], masks, chains, embed, in_gain[0:1, :], in_bias[0:1, :],
            (r ^ 3) * rows, first, count,
        )
        zm = zn * spread.astype(BF16)
        right = gated_side(zm, weights, 0, 1, chan)
        for j in range(count):
            late_ref[pl.ds(first_late + first + j, n, stride=late), :] = right[j * n : (j + 1) * n]
        at = pl.ds(first * n, size)
        zf_ref[at, :] = z
        mf_ref[at, :] = spread
        zn_ref[at, :] = zn.astype(F32)

    own = pl.ds(pl.multiple_of(core * mid, 8), mid)
    tail = pl.ds(block + mid, mid)
    zn = zn_ref[own, :].astype(BF16)
    spread = mf_ref[own, :]
    left_ref[tail, :] = gated_side(zn * spread.astype(BF16), weights, 0, 0, chan)
    z_ref[tail, :] = zf_ref[own, :]
    g_ref[tail, :] = jax.nn.sigmoid(nn_dot(zn, gate_w[0]))
    m_ref[tail, :] = spread
    head = pl.ds(0, block + mid)
    left_ref[head, :] = left_in[...]
    z_ref[head, :] = z_in[...]
    g_ref[head, :] = g_in[...]
    m_ref[head, :] = m_in[...]

    group = rows // 2
    x_ref[head, :] = x_in[...]
    for i, acc in enumerate(
        tiles_of(n, group, lambda i: block + mid + i * n, left_ref, 1, n, right_in, 0, early, n)
    ):
        x_ref[pl.ds(block + mid + i * n, early), :] = acc
    for t in range(2):
        for i, acc in enumerate(
            tiles_of(n, rows, lambda i: t * block + i * n, left_ref, 1, n, late_ref, 0, late, late)
        ):
            x_ref[pl.ds(t * block + i * n + early, late), :] = acc

    def ordered(first, count):
        out = []
        for i in range(first, first + count):
            for b in range(4):
                out.append(x_ref[pl.ds(i * n + (r ^ b) * rows, rows), :])
        return jnp.concatenate(out, axis=0)

    for first, count in pieces(2 * rows, 8):
        at = pl.ds(first * n, count * n)
        update = hidden_update(ordered(first, count), out_gain[0:1, :], out_bias[0:1, :], out_w[0])
        z1 = (z_ref[at, :] + g_ref[at, :] * update).astype(BF16)
        z1_ref[at, :] = z1
        own_count = max(0, min(count, rows - first))
        if own_count:
            own_ref[pl.ds(first * n, own_count * n), :] = z1[: own_count * n]


def hidden_update(x, gain, bias, weight):
    mean = jnp.mean(x, axis=-1, keepdims=True)
    meansq = jnp.mean(x * x, axis=-1, keepdims=True)
    scale = lax.rsqrt(meansq - mean * mean + EPS)
    return nn_dot(((x - mean) * scale * gain + bias).astype(BF16), weight)


def incoming_kernel(n, rows, z1, masks, weights, in_gain, in_bias, part, left_ref, right_ref, sums_ref):
    r = lax.axis_index("row")
    chan = z1.shape[1]
    for first, count in pieces(2 * rows, 8):
        at = pl.ds(first * n, count * n)
        zn = normalize(z1[at, :].astype(F32), in_gain[1:2, :], in_bias[1:2, :])
        zm = zn * masks[at, :].astype(BF16)
        left_ref[at, :] = gated_side(zm, weights, 1, 0, chan)
        right_ref[at, :] = gated_side(zm, weights, 1, 1, chan)
    group = rows // 2
    wide = (n // 8 + 1) // 2 * 8
    for t in range(2):
        start = r * rows + t * group
        sums = [
            tiles_of(n, group, lambda i: start + i, left_ref, n, 2 * rows, right_ref, at, width, n)
            for at, width in ((0, wide), (wide, n - wide))
        ]
        for i in range(group):
            for (at, width), accs in zip(((0, wide), (wide, n - wide)), sums):
                left = (t * group + i) * n + at
                sums_ref[left : left + width, :] = accs[i]
    part[...] = sums_ref[...].astype(BF16)


def gate_kernel(own, received, in_gain, in_bias, gate_w, z_ref, g_ref):
    even = lax.rem(lax.axis_index("ch"), 2) == 0
    z = jnp.where(even, own[...], received[...]).astype(F32)
    z_ref[...] = z
    zn = normalize(z, in_gain[1:2, :], in_bias[1:2, :])
    g_ref[...] = jax.nn.sigmoid(nn_dot(zn, gate_w[1]))


def last_kernel(n, rows, part, received, z_ref, g_ref, out_gain, out_bias, out_w, result):
    for first, count in pieces(rows, 8):
        at = pl.ds(first * n, count * n)
        x = part[at, :].astype(F32) + received[at, :].astype(F32)
        update = hidden_update(x, out_gain[1:2, :], out_bias[1:2, :], out_w[1])
        out = (z_ref[at, :] + g_ref[at, :] * update).astype(BF16)
        for i in range(count):
            result[first + i] = out[i * n : (i + 1) * n]


def in_one_phase(
    pair, chain_ids, mask, pair_embed, in_gain, in_bias, proj_weight, gate_weight, out_gain, out_bias, out_weight
):
    rows, n, chan = pair.shape
    hid = proj_weight.shape[3]
    size = 8 * hid
    block, mid = rows * n, rows // 2 * n
    flat_pair = pair.reshape(block, chan)
    weights = jnp.transpose(proj_weight, (0, 1, 3, 2)).reshape(size, chan)
    part = (block // 2 + 15) // 16 * 16
    early = 3 * rows // 8 * 8
    both = ("row", "ch")
    vmem = pl.BlockSpec(memory_space=pltpu.VMEM)

    def pairs_of(source):
        return [(source(r, c), r * 4 + c) for r in range(4) for c in range(4)]

    first = pairs_of(lambda r, c: (r ^ (1 + c % 2)) * 4 + c)
    second = pairs_of(lambda r, c: (r ^ 3) * 4 + c)
    cores = [(c, c ^ 1) for c in range(4)]
    chips = [(c, c ^ 2) for c in range(4)]

    def call(kernel, name, outs, ins, scratch=(), us=1.0):
        kept = [pltpu.with_memory_space_constraint(v, pltpu.VMEM) if id(v) in in_vmem else v for v in ins]
        got = pl.pallas_call(
            kernel,
            out_shape=tuple(outs),
            in_specs=[vmem] * len(ins),
            out_specs=tuple(vmem for _ in outs),
            scratch_shapes=[pltpu.VMEM(s, F32) for s in scratch],
            compiler_params=pltpu.CompilerParams(vmem_limit_bytes=32 * 1024 * 1024),
            cost_estimate=pl.CostEstimate(flops=int(us * 1.2e9), bytes_accessed=0, transcendentals=0),
            name=name,
        )(*kept)
        for v in got:
            in_vmem[id(v)] = v
        return got

    in_vmem = {}
    f32 = lambda count: pltpu.VMEM((count, chan), F32)
    bf16 = lambda count: pltpu.VMEM((count, chan), BF16)

    hbm = pl.BlockSpec(memory_space=pl.ANY)
    (packed,) = pl.pallas_call(
        functools.partial(pack_kernel, n, rows),
        out_shape=(bf16(block + MASK_ROWS),),
        in_specs=[hbm] * 2,
        out_specs=(vmem,),
        scratch_shapes=[pltpu.VMEM((rows, n), jnp.int32), pltpu.SemaphoreType.DMA((2,))],
        name="pack",
    )(*(pltpu.with_memory_space_constraint(v, pltpu.HBM) for v in (flat_pair, mask)))
    sources = (weights, pair_embed, in_gain, in_bias, gate_weight, out_gain, out_bias, out_weight)
    constants = pl.pallas_call(
        functools.partial(constants_kernel, part),
        out_shape=tuple(pltpu.VMEM(v.shape, v.dtype) for v in sources) + (f32(n), bf16(part + MASK_ROWS)),
        in_specs=[vmem] + [hbm] * (1 + len(sources)),
        out_specs=(vmem,) * (2 + len(sources)),
        scratch_shapes=[pltpu.VMEM((1, n), jnp.int32), pltpu.SemaphoreType.DMA((1 + len(sources),))],
        cost_estimate=pl.CostEstimate(flops=10**7, bytes_accessed=0, transcendentals=0),
        name="constants",
    )(
        pltpu.with_memory_space_constraint(packed, pltpu.VMEM),
        *(pltpu.with_memory_space_constraint(v, pltpu.HBM) for v in (chain_ids.reshape(1, n),) + sources),
    )
    in_vmem.update({id(v): v for v in (packed,) + tuple(constants)})
    w_own, pair_embed, in_gain, in_bias, gate_weight, out_gain, out_bias, out_weight, chains, halved = constants
    packed_a = lax.ppermute(packed, both, first)
    half_b = lax.ppermute(halved, both, second)
    w_e = lax.ppermute(weights, "ch", cores)
    w_a = lax.ppermute(weights, "ch", chips)
    w_f = lax.ppermute(w_a, "ch", cores)
    def one_block(name, which, source):
        return call(
            functools.partial(lift_kernel, n, rows, which),
            name,
            [f32(block)] * 3 + [bf16(block)],
            [source, chains, pair_embed, in_gain, in_bias, gate_weight],
            us=0.8,
        )

    at_o = one_block("lift_own", lambda core: 0, packed)
    (w_all,) = call(weights_kernel, "weights", [bf16(4 * size)], [w_own, w_e, w_a, w_f], us=0.1)

    def project(name, lifted):
        sides = call(functools.partial(project_kernel, n, rows), name, [f32(block)] * 2, [lifted[3], w_all], us=0.6)
        return list(lifted[:3]) + list(sides)

    (packed_a,) = call(pass_kernel, "pass_first", [bf16(block + MASK_ROWS)], [packed_a, at_o[0]], us=0.1)
    at_o = project("project_own", at_o)
    packed_e = lax.ppermute(packed_a, "ch", cores)
    at_a = one_block("lift_first", lambda core: 1 + core, packed_a)
    at_e = one_block("lift_second", lambda core: 2 - core, packed_e)
    at_a, at_e = (project(name, v) for name, v in (("project_first", at_a), ("project_second", at_e)))
    (half_b,) = call(pass_kernel, "pass_on", [bf16(part + MASK_ROWS)], [half_b, at_e[4]], us=0.1)
    half_f = lax.ppermute(half_b, "ch", cores)
    at_early = call(
        functools.partial(early_kernel, n, rows, early),
        "early",
        [f32(block + mid), f32(n * n)] + [f32(block + mid)] * 4,
        [v for three in zip(at_o, at_a, at_e) for v in three],
        us=2.0,
    )
    z1, own, masks = call(
        functools.partial(late_kernel, n, rows, part, early),
        "late",
        [bf16(2 * block), bf16(block), f32(2 * block)],
        [half_b, half_f, w_all, chains, pair_embed, in_gain, in_bias, gate_weight, out_gain, out_bias, out_weight]
        + list(at_early),
        [(2 * block, chan), (n * (n - early), chan)] + [(2 * block, chan)] * 3 + [(block, chan)] * 3,
        us=4.0,
    )
    own_n = lax.ppermute(own, "ch", cores)
    (part,) = call(
        functools.partial(incoming_kernel, n, rows),
        "incoming",
        [bf16(block)],
        [z1, masks, w_all, in_gain, in_bias],
        scratch=[(2 * block, chan)] * 2 + [(block, chan)],
        us=3.0,
    )
    part_n = lax.ppermute(part, "ch", cores)
    z1_own, gate = call(gate_kernel, "gate", [f32(block)] * 2, [own, own_n, in_gain, in_bias, gate_weight])
    (result,) = call(
        functools.partial(last_kernel, n, rows),
        "last",
        [jax.ShapeDtypeStruct((rows, n, chan), BF16)],
        [part, part_n, z1_own, gate, out_gain, out_bias, out_weight],
    )
    return result


def layer_norm(values, gain, bias):
    mean = jnp.mean(values, axis=-1, keepdims=True)
    centered = values - mean
    var = jnp.mean(centered * centered, axis=-1, keepdims=True)
    return centered * lax.rsqrt(var + EPS) * gain + bias


def gated(normed, weights, maskf, form):
    proj = jnp.einsum(form, normed, weights, preferred_element_type=jnp.float32)
    return (jax.nn.sigmoid(proj[0]) * proj[1] * maskf).astype(jnp.bfloat16)


def outgoing(normed, weights, maskf):
    left = gated(normed, weights[0:2], maskf, "rnc,qch->qhrn")
    right = gated(normed, weights[2:4], maskf, "rnc,qch->qhrn")
    return jnp.einsum(
        "hik,hjk->hij",
        left,
        lax.all_gather(right, "row", axis=1, tiled=True),
        preferred_element_type=jnp.float32,
    ).astype(jnp.bfloat16)


def incoming(normed, weights, maskf):
    right = gated(normed, weights[2:4], maskf, "rnc,qch->qhrn")
    left = gated(normed, weights[0:2], maskf, "rnc,qch->qhrn")
    summed = jnp.transpose(
        lax.psum_scatter(
            jnp.einsum("hki,hkj->ihj", left, right, preferred_element_type=jnp.float32),
            "row",
            scatter_dimension=0,
            tiled=True,
        ),
        (1, 0, 2),
    )
    return summed.astype(jnp.bfloat16)


def finish(mixed, layer, out_gain, out_bias, out_weight):
    hid_full = out_weight.shape[1]
    whole = lax.all_gather(mixed, "ch", axis=0, tiled=True)
    values = whole.astype(jnp.float32)
    mean = jnp.sum(values, axis=0) / hid_full
    meansq = jnp.sum(values * values, axis=0) / hid_full
    gain = out_gain[layer]
    bias = out_bias[layer]
    weight = out_weight[layer]
    scale = lax.rsqrt(meansq - mean * mean + EPS)
    hidden = ((values - mean) * scale * gain[:, None, None] + bias[:, None, None]).astype(
        jnp.bfloat16
    )
    update = jnp.einsum("hrn,hc->rnc", hidden, weight, preferred_element_type=jnp.float32)
    return update


def fits(pair_shape, weight_shape):
    rows, n, chan = pair_shape
    hid = weight_shape[3]
    return (
        lax.axis_size("row") == 4
        and lax.axis_size("ch") == 4
        and rows * 4 == n
        and rows <= MASK_ROWS
        and rows % 2 == 0
        and n % 8 == 0
        and n <= chan
        and hid % 16 == 0
        and hid * 4 == chan
        and chan % 128 == 0
        and n * n * chan * 4 * 6 <= 16 * 1024 * 1024
    )


def per_device(
    pair,
    chain_ids,
    mask,
    pair_embed,
    in_gain,
    in_bias,
    proj_weight,
    gate_weight,
    out_gain,
    out_bias,
    out_weight,
):
    rows = pair.shape[0]
    if fits(pair.shape, proj_weight.shape):
        return in_one_phase(
            pair, chain_ids, mask, pair_embed, in_gain, in_bias, proj_weight, gate_weight, out_gain, out_bias, out_weight
        )
    start_row = lax.axis_index("row") * rows
    own_chain = lax.dynamic_slice_in_dim(chain_ids, start_row, rows, 0)
    same = (own_chain[:, None] == chain_ids[None, :])[:, :, None]
    current = pair.astype(jnp.float32) + jnp.where(same, pair_embed[1], pair_embed[0])
    maskf = mask.astype(jnp.float32)
    result = pair
    for layer in range(2):
        normed = layer_norm(current, in_gain[layer], in_bias[layer]).astype(jnp.bfloat16)
        weights = proj_weight[layer]
        if layer == 0:
            mixed = outgoing(normed, weights, maskf)
        else:
            mixed = incoming(normed, weights, maskf)
        update = finish(mixed, layer, out_gain, out_bias, out_weight)
        gate = jax.nn.sigmoid(
            jnp.dot(normed, gate_weight[layer], preferred_element_type=jnp.float32)
        )
        result = lax.optimization_barrier((current + gate * update).astype(jnp.bfloat16))
        current = result.astype(jnp.float32)
    return result


def solution(mesh):
    placed = (
        P(("grp", "row"), None, None),
        P("grp"),
        P(("grp", "row"), None),
        P(),
        P(),
        P(),
        P(None, None, None, "ch"),
        P(),
        P(),
        P(),
        P(),
    )
    return jax.shard_map(
        per_device,
        mesh=mesh,
        in_specs=placed,
        out_specs=P(("grp", "row"), None, None),
        check_vma=False,
    )
```

```python
import functools

import jax
import jax.numpy as jnp
from jax import lax
from jax.experimental import pallas as pl
from jax.experimental.pallas import tpu as pltpu
from jax.sharding import PartitionSpec as P

EPS = 1e-05
F32 = jnp.float32
BF16 = jnp.bfloat16
MASK_ROWS = 16


def nt_dot(a, b):
    return lax.dot_general(a, b, (((1,), (1,)), ((), ())), preferred_element_type=F32)


def nn_dot(a, b):
    return lax.dot_general(a, b, (((1,), (0,)), ((), ())), preferred_element_type=F32)


def half_sigmoid(half):
    return 0.5 * jnp.tanh(half) + 0.5


def normalize(values, gain, bias):
    mean = jnp.mean(values, axis=-1, keepdims=True)
    centered = values - mean
    var = jnp.mean(centered * centered, axis=-1, keepdims=True)
    return (centered * lax.rsqrt(var + EPS) * gain + bias).astype(BF16)


def pieces(rows, most):
    out, first = [], 0
    while first < rows:
        count = min(most, rows - first)
        out.append((first, count))
        first += count
    return out


def spread_masks(mask, rows, n, chan):
    spread = (
        lax.broadcasted_iota(jnp.int32, (rows, rows * chan), 1) // chan
        == lax.broadcasted_iota(jnp.int32, (rows, rows * chan), 0)
    ).astype(BF16)
    return lax.dot_general(mask.astype(BF16), spread, (((0,), (0,)), ((), ())), preferred_element_type=F32)


def lift(pair_rows, masks, chains, embed, gain, bias, position, first, count):
    other, same = embed[0:1, :], embed[1:2, :]
    chan = chains.shape[1]
    z = jnp.concatenate(
        [
            jnp.where(chains[...] == chains[pl.ds(position + i, 1), :], same, other)
            for i in range(first, first + count)
        ],
        axis=0,
    ) + pair_rows.astype(F32)
    spread = jnp.concatenate([masks[:, i * chan : (i + 1) * chan] for i in range(first, first + count)], axis=0)
    return z, normalize(z, gain, bias), spread


def gated_side(zm, weights, u, side, chan):
    base = (u * 4 + side * 2) * chan
    both = nt_dot(zm, weights[base : base + 2 * chan, :])
    return (jnp.tanh(both[:, :chan]) + 1.0) * both[:, chan:]


def pack_kernel(n, rows, pair, mask, packed, mask_v, sems):
    block, chan = pair.shape
    copies = [
        pltpu.make_async_copy(mask, mask_v, sems.at[0]),
        pltpu.make_async_copy(pair, packed.at[pl.ds(0, block)], sems.at[1]),
    ]
    for copy in copies:
        copy.start()
    copies[0].wait()
    wide = jnp.concatenate([mask_v[...].astype(F32), jnp.zeros((rows, chan - n), F32)], axis=1)
    packed[block : block + MASK_ROWS, :] = jnp.concatenate(
        [wide, jnp.zeros((MASK_ROWS - rows, chan), F32)], axis=0
    ).astype(BF16)
    copies[1].wait()


def constants_kernel(part, packed, chain_row, *refs):
    count = (len(refs) - 4) // 2
    sources, outs = refs[:count], refs[count : 2 * count]
    chains, halved, row, sems = refs[2 * count :]
    first = pltpu.make_async_copy(chain_row, row, sems.at[count])
    first.start()
    copies = [pltpu.make_async_copy(a, b, sems.at[i]) for i, (a, b) in enumerate(zip(sources, outs))]
    for copy in copies:
        copy.start()
    core = lax.rem(lax.axis_index("ch"), 2)
    block = packed.shape[0] - MASK_ROWS
    start = pl.multiple_of(core * (block - part), 16)
    halved[0:part, :] = packed[pl.ds(start, part), :]
    halved[part : part + MASK_ROWS, :] = packed[block : block + MASK_ROWS, :]
    first.wait()
    ones = jnp.ones((1, chains.shape[1]), BF16)
    chains[...] = lax.dot_general(
        row[...].astype(F32).astype(BF16), ones, (((0,), (0,)), ((), ())), preferred_element_type=F32
    )
    for copy in copies:
        copy.wait()


def pass_kernel(value, after, out):
    out[...] = value[...]


def weights_kernel(w_o, w_e, w_a, w_f, weights):
    c = lax.axis_index("ch")
    hid = w_e.shape[0] // 8
    for at, ref in enumerate((w_o, w_e, w_a, w_f)):
        for q in range(8):
            first = pl.multiple_of(q * 4 * hid + (c ^ at) * hid, 16)
            weights[pl.ds(first, hid), :] = ref[q * hid : (q + 1) * hid, :] * jnp.asarray(0.5, BF16)


def lift_kernel(
    n, rows, which,
    packed, chains, embed, in_gain, in_bias, gate_w,
    z_ref, g_ref, m_ref, zm_ref,
):
    r = lax.axis_index("row")
    core = lax.rem(lax.axis_index("ch"), 2)
    position = (r ^ which(core)) * rows
    chan = packed.shape[1]
    masks_at = packed.shape[0] - MASK_ROWS
    masks = spread_masks(packed[masks_at : masks_at + MASK_ROWS, 0:n][0:rows], rows, n, chan)
    for first, count in pieces(rows, 8):
        at = pl.ds(first * n, count * n)
        z, zn, spread = lift(
            packed[at, :], masks, chains, embed, in_gain[0:1, :], in_bias[0:1, :], position, first, count
        )
        z_ref[at, :] = z
        m_ref[at, :] = spread
        g_ref[at, :] = half_sigmoid(0.5 * nn_dot(zn, gate_w[0]))
        zm_ref[at, :] = zn * spread.astype(BF16)


def project_kernel(n, rows, zm_ref, weights, left_ref, right_ref):
    chan = zm_ref.shape[1]
    for first, count in pieces(rows, 8):
        at = pl.ds(first * n, count * n)
        zm = zm_ref[at, :]
        left_ref[at, :] = gated_side(zm, weights, 0, 0, chan)
        right_ref[at, :] = gated_side(zm, weights, 0, 1, chan)


def tiles_of(lefts, steps, right_ref, right_at, width, right_step):
    chan = right_ref.shape[1]

    def body(k, accs):
        right = right_ref[pl.ds(pl.multiple_of(right_at + k * right_step, 8), width), :]
        return tuple(acc + ref[pl.ds(at + k * step, 1), :] * right for acc, (ref, at, step) in zip(accs, lefts))

    zeros = tuple(jnp.zeros((width, chan), F32) for _ in lefts)
    return lax.fori_loop(0, steps, body, zeros, unroll=min(28, steps))


def early_kernel(
    n, rows, early, left_o, left_a, left_e, right_o, right_a, right_e, x_ref, right_ref, left_ref,
):
    core = lax.rem(lax.axis_index("ch"), 2)
    block, mid = rows * n, rows // 2 * n

    @pl.when(core == 0)
    def _():
        left_ref[0:block, :] = left_o[...]
        left_ref[block : block + mid, :] = left_a[0:mid, :]

    @pl.when(core == 1)
    def _():
        left_ref[0:block, :] = left_a[...]
        left_ref[block : block + mid, :] = left_e[mid:block, :]

    for j in range(rows):
        rows_of_j = slice(j * n, (j + 1) * n)
        right_ref[pl.ds(j, n, stride=n), :] = right_o[rows_of_j, :]
        right_ref[pl.ds(rows * (1 + core) + j, n, stride=n), :] = right_a[rows_of_j, :]
        right_ref[pl.ds(rows * (2 - core) + j, n, stride=n), :] = right_e[rows_of_j, :]

    group = rows // 2

    def some(t, _):
        first = t * group * n
        accs = tiles_of([(left_ref, first + i * n, 1) for i in range(group)], n, right_ref, 0, early, n)
        for i, acc in enumerate(accs):
            x_ref[pl.ds(pl.multiple_of(first + i * n, 8), early), :] = acc
        return 0

    lax.fori_loop(0, 3, some, 0)


def late_kernel(
    n, rows, part, early,
    half_b, half_f, weights, chains, embed, in_gain, in_bias, gate_w, out_gain, out_bias, out_w,
    x_in, right_in, left_in, z_o, z_a, z_e, g_o, g_a, g_e,
    z1_ref, own_ref, m_ref,
    x_ref, late_ref, left_ref, zn_ref, mf_ref, zf_ref,
):
    r = lax.axis_index("row")
    core = lax.rem(lax.axis_index("ch"), 2)
    even = core == 0
    block, mid = rows * n, rows // 2 * n
    chan = half_b.shape[1]
    late = n - early
    masks = spread_masks(half_b[part : part + MASK_ROWS, 0:n][0:rows], rows, n, chan)
    skip = 2 * part - block
    pair_rows = jnp.concatenate(
        [
            jnp.where(even, half_b[0:part, :], half_f[0:part, :]),
            jnp.where(even, half_f[skip:part, :], half_b[skip:part, :]),
        ],
        axis=0,
    )

    first_late = 3 * rows - early
    for t in range(first_late):
        late_ref[pl.ds(t, n, stride=late), :] = right_in[pl.ds(early + t, n, stride=n), :]
    for first, count in pieces(rows, 8):
        size = count * n
        z, zn, spread = lift(
            pair_rows[first * n : first * n + size], masks, chains, embed, in_gain[0:1, :], in_bias[0:1, :],
            (r ^ 3) * rows, first, count,
        )
        zm = zn * spread.astype(BF16)
        right = gated_side(zm, weights, 0, 1, chan)
        for j in range(count):
            late_ref[pl.ds(first_late + first + j, n, stride=late), :] = right[j * n : (j + 1) * n]
        at = pl.ds(first * n, size)
        zf_ref[at, :] = z
        mf_ref[at, :] = spread
        zn_ref[at, :] = zn.astype(F32)

    own = pl.ds(pl.multiple_of(core * mid, 8), mid)
    zn = zn_ref[own, :].astype(BF16)
    spread = mf_ref[own, :]
    left_ref[...] = gated_side(zn * spread.astype(BF16), weights, 0, 0, chan)
    m_ref[...] = spread

    group = rows // 2
    head = block + mid
    x_ref[0:head, :] = x_in[...]
    tail_lefts = [(left_ref, i * n, 1) for i in range(group)]
    for i, acc in enumerate(tiles_of(tail_lefts, n, right_in, 0, early, n)):
        x_ref[head + i * n : head + i * n + early, :] = acc
    lefts = [(left_in, i * n, 1) for i in range(3 * group)] + tail_lefts
    for t in range(2):
        for i, acc in enumerate(tiles_of(lefts[t * rows : (t + 1) * rows], n, late_ref, 0, late, late)):
            row = t * block + i * n + early
            x_ref[row : row + late, :] = acc

    def finish(first, count, z, gate):
        x = jnp.concatenate(
            [
                x_ref[pl.ds(i * n + (r ^ b) * rows, rows), :]
                for i in range(first, first + count)
                for b in range(4)
            ],
            axis=0,
        )
        update = hidden_update(x, out_gain[0:1, :], out_bias[0:1, :], out_w[0])
        z1 = (z + gate * update).astype(BF16)
        z1_ref[first * n : (first + count) * n, :] = z1.astype(F32)
        return z1

    for first, count in pieces(rows, 8):
        at = slice(first * n, (first + count) * n)
        own_ref[at, :] = finish(
            first, count, jnp.where(even, z_o[at, :], z_a[at, :]), jnp.where(even, g_o[at, :], g_a[at, :])
        )
    finish(
        rows, group,
        jnp.where(even, z_a[0:mid, :], z_e[mid:block, :]), jnp.where(even, g_a[0:mid, :], g_e[mid:block, :]),
    )
    finish(rows + group, group, zf_ref[own, :], half_sigmoid(0.5 * nn_dot(zn, gate_w[0])))


def hidden_update(x, gain, bias, weight):
    mean = jnp.mean(x, axis=-1, keepdims=True)
    meansq = jnp.mean(x * x, axis=-1, keepdims=True)
    scale = lax.rsqrt(meansq - mean * mean + EPS)
    return nn_dot(((x - mean) * scale * gain + bias).astype(BF16), weight)


def incoming_kernel(
    n, rows, z1, m_o, m_a, m_e, m_f, weights, in_gain, in_bias, part, left_ref, right_ref, sums_ref
):
    r = lax.axis_index("row")
    even = lax.rem(lax.axis_index("ch"), 2) == 0
    chan = z1.shape[1]
    block, mid = rows * n, rows // 2 * n
    group = rows // 2
    kept = [
        (first, count, lambda at: jnp.where(even, m_o[at, :], m_a[at, :])) for first, count in pieces(rows, 8)
    ]
    kept.append((rows, group, lambda at: jnp.where(even, m_a[0:mid, :], m_e[mid:block, :])))
    kept.append((rows + group, group, lambda at: m_f[...]))
    for first, count, masks in kept:
        at = slice(first * n, (first + count) * n)
        zn = normalize(z1[at, :], in_gain[1:2, :], in_bias[1:2, :])
        zm = zn * masks(at).astype(BF16)
        left_ref[at, :] = gated_side(zm, weights, 1, 0, chan)
        right_ref[at, :] = gated_side(zm, weights, 1, 1, chan)
    wide = (n // 8 + 1) // 2 * 8
    for t in range(2):
        start = r * rows + t * group
        for at, width in ((0, wide), (wide, n - wide)):
            accs = tiles_of([(left_ref, start + i, n) for i in range(group)], 2 * rows, right_ref, at, width, n)
            for i, acc in enumerate(accs):
                row = (t * group + i) * n + at
                sums_ref[row : row + width, :] = acc
    part[...] = sums_ref[...].astype(BF16)


def gate_kernel(own, received, in_gain, in_bias, gate_w, z_ref, g_ref):
    even = lax.rem(lax.axis_index("ch"), 2) == 0
    z = jnp.where(even, own[...], received[...]).astype(F32)
    z_ref[...] = z
    zn = normalize(z, in_gain[1:2, :], in_bias[1:2, :])
    g_ref[...] = half_sigmoid(0.5 * nn_dot(zn, gate_w[1]))


def last_kernel(n, rows, part, received, z_ref, g_ref, out_gain, out_bias, out_w, result):
    for first, count in pieces(rows, 8):
        at = pl.ds(first * n, count * n)
        x = part[at, :].astype(F32) + received[at, :].astype(F32)
        update = hidden_update(x, out_gain[1:2, :], out_bias[1:2, :], out_w[1])
        out = (z_ref[at, :] + g_ref[at, :] * update).astype(BF16)
        for i in range(count):
            result[first + i] = out[i * n : (i + 1) * n]


def in_one_phase(
    pair, chain_ids, mask, pair_embed, in_gain, in_bias, proj_weight, gate_weight, out_gain, out_bias, out_weight
):
    rows, n, chan = pair.shape
    hid = proj_weight.shape[3]
    size = 8 * hid
    block, mid = rows * n, rows // 2 * n
    flat_pair = pair.reshape(block, chan)
    weights = jnp.transpose(proj_weight, (0, 1, 3, 2)).reshape(size, chan)
    part = (block // 2 + 15) // 16 * 16
    early = 3 * rows // 8 * 8
    both = ("row", "ch")
    vmem = pl.BlockSpec(memory_space=pltpu.VMEM)

    def pairs_of(source):
        return [(source(r, c), r * 4 + c) for r in range(4) for c in range(4)]

    first = pairs_of(lambda r, c: (r ^ (1 + c % 2)) * 4 + c)
    second = pairs_of(lambda r, c: (r ^ 3) * 4 + c)
    cores = [(c, c ^ 1) for c in range(4)]
    chips = [(c, c ^ 2) for c in range(4)]

    def call(kernel, name, outs, ins, scratch=(), us=1.0):
        kept = [pltpu.with_memory_space_constraint(v, pltpu.VMEM) if id(v) in in_vmem else v for v in ins]
        got = pl.pallas_call(
            kernel,
            out_shape=tuple(outs),
            in_specs=[vmem] * len(ins),
            out_specs=tuple(vmem for _ in outs),
            scratch_shapes=[pltpu.VMEM(s, F32) for s in scratch],
            compiler_params=pltpu.CompilerParams(vmem_limit_bytes=32 * 1024 * 1024),
            cost_estimate=pl.CostEstimate(flops=int(us * 1.2e9), bytes_accessed=0, transcendentals=0),
            name=name,
        )(*kept)
        for v in got:
            in_vmem[id(v)] = v
        return got

    in_vmem = {}
    f32 = lambda count: pltpu.VMEM((count, chan), F32)
    bf16 = lambda count: pltpu.VMEM((count, chan), BF16)

    hbm = pl.BlockSpec(memory_space=pl.ANY)
    (packed,) = pl.pallas_call(
        functools.partial(pack_kernel, n, rows),
        out_shape=(bf16(block + MASK_ROWS),),
        in_specs=[hbm] * 2,
        out_specs=(vmem,),
        scratch_shapes=[pltpu.VMEM((rows, n), jnp.int32), pltpu.SemaphoreType.DMA((2,))],
        name="pack",
    )(*(pltpu.with_memory_space_constraint(v, pltpu.HBM) for v in (flat_pair, mask)))
    sources = (weights, pair_embed, in_gain, in_bias, gate_weight, out_gain, out_bias, out_weight)
    constants = pl.pallas_call(
        functools.partial(constants_kernel, part),
        out_shape=tuple(pltpu.VMEM(v.shape, v.dtype) for v in sources) + (f32(n), bf16(part + MASK_ROWS)),
        in_specs=[vmem] + [hbm] * (1 + len(sources)),
        out_specs=(vmem,) * (2 + len(sources)),
        scratch_shapes=[pltpu.VMEM((1, n), jnp.int32), pltpu.SemaphoreType.DMA((1 + len(sources),))],
        cost_estimate=pl.CostEstimate(flops=10**7, bytes_accessed=0, transcendentals=0),
        name="constants",
    )(
        pltpu.with_memory_space_constraint(packed, pltpu.VMEM),
        *(pltpu.with_memory_space_constraint(v, pltpu.HBM) for v in (chain_ids.reshape(1, n),) + sources),
    )
    in_vmem.update({id(v): v for v in (packed,) + tuple(constants)})
    w_own, pair_embed, in_gain, in_bias, gate_weight, out_gain, out_bias, out_weight, chains, halved = constants
    packed_a = lax.ppermute(packed, both, first)
    half_b = lax.ppermute(halved, both, second)
    w_e = lax.ppermute(weights, "ch", cores)
    w_a = lax.ppermute(weights, "ch", chips)
    w_f = lax.ppermute(w_a, "ch", cores)
    def one_block(name, which, source):
        return call(
            functools.partial(lift_kernel, n, rows, which),
            name,
            [f32(block)] * 3 + [bf16(block)],
            [source, chains, pair_embed, in_gain, in_bias, gate_weight],
            us=0.8,
        )

    at_o = one_block("lift_own", lambda core: 0, packed)
    (w_all,) = call(weights_kernel, "weights", [bf16(4 * size)], [w_own, w_e, w_a, w_f], us=0.1)

    def project(name, lifted):
        sides = call(functools.partial(project_kernel, n, rows), name, [f32(block)] * 2, [lifted[3], w_all], us=0.6)
        return list(lifted[:3]) + list(sides)

    (packed_a,) = call(pass_kernel, "pass_first", [bf16(block + MASK_ROWS)], [packed_a, at_o[0]], us=0.1)
    at_o = project("project_own", at_o)
    packed_e = lax.ppermute(packed_a, "ch", cores)
    at_a = one_block("lift_first", lambda core: 1 + core, packed_a)
    at_e = one_block("lift_second", lambda core: 2 - core, packed_e)
    at_a, at_e = (project(name, v) for name, v in (("project_first", at_a), ("project_second", at_e)))
    (half_b,) = call(pass_kernel, "pass_on", [bf16(part + MASK_ROWS)], [half_b, at_e[4]], us=0.1)
    half_f = lax.ppermute(half_b, "ch", cores)
    x, right, left = call(
        functools.partial(early_kernel, n, rows, early),
        "early",
        [f32(block + mid), f32(n * n), f32(block + mid)],
        [at_o[3], at_a[3], at_e[3], at_o[4], at_a[4], at_e[4]],
        us=2.0,
    )
    z1, own, mask_f = call(
        functools.partial(late_kernel, n, rows, part, early),
        "late",
        [f32(2 * block), bf16(block), f32(mid)],
        [half_b, half_f, w_all, chains, pair_embed, in_gain, in_bias, gate_weight, out_gain, out_bias, out_weight]
        + [x, right, left]
        + [v[at] for at in (0, 1) for v in (at_o, at_a, at_e)],
        [(2 * block, chan), (n * (n - early), chan), (mid, chan)] + [(block, chan)] * 3,
        us=4.0,
    )
    own_n = lax.ppermute(own, "ch", cores)
    (part,) = call(
        functools.partial(incoming_kernel, n, rows),
        "incoming",
        [bf16(block)],
        [z1, at_o[2], at_a[2], at_e[2], mask_f, w_all, in_gain, in_bias],
        scratch=[(2 * block, chan)] * 2 + [(block, chan)],
        us=3.0,
    )
    part_n = lax.ppermute(part, "ch", cores)
    z1_own, gate = call(gate_kernel, "gate", [f32(block)] * 2, [own, own_n, in_gain, in_bias, gate_weight])
    (result,) = call(
        functools.partial(last_kernel, n, rows),
        "last",
        [jax.ShapeDtypeStruct((rows, n, chan), BF16)],
        [part, part_n, z1_own, gate, out_gain, out_bias, out_weight],
    )
    return result


def layer_norm(values, gain, bias):
    mean = jnp.mean(values, axis=-1, keepdims=True)
    centered = values - mean
    var = jnp.mean(centered * centered, axis=-1, keepdims=True)
    return centered * lax.rsqrt(var + EPS) * gain + bias


def gated(normed, weights, maskf, form):
    proj = jnp.einsum(form, normed, weights, preferred_element_type=jnp.float32)
    return (jax.nn.sigmoid(proj[0]) * proj[1] * maskf).astype(jnp.bfloat16)


def outgoing(normed, weights, maskf):
    left = gated(normed, weights[0:2], maskf, "rnc,qch->qhrn")
    right = gated(normed, weights[2:4], maskf, "rnc,qch->qhrn")
    return jnp.einsum(
        "hik,hjk->hij",
        left,
        lax.all_gather(right, "row", axis=1, tiled=True),
        preferred_element_type=jnp.float32,
    ).astype(jnp.bfloat16)


def incoming(normed, weights, maskf):
    right = gated(normed, weights[2:4], maskf, "rnc,qch->qhrn")
    left = gated(normed, weights[0:2], maskf, "rnc,qch->qhrn")
    summed = jnp.transpose(
        lax.psum_scatter(
            jnp.einsum("hki,hkj->ihj", left, right, preferred_element_type=jnp.float32),
            "row",
            scatter_dimension=0,
            tiled=True,
        ),
        (1, 0, 2),
    )
    return summed.astype(jnp.bfloat16)


def finish(mixed, layer, out_gain, out_bias, out_weight):
    hid_full = out_weight.shape[1]
    whole = lax.all_gather(mixed, "ch", axis=0, tiled=True)
    values = whole.astype(jnp.float32)
    mean = jnp.sum(values, axis=0) / hid_full
    meansq = jnp.sum(values * values, axis=0) / hid_full
    gain = out_gain[layer]
    bias = out_bias[layer]
    weight = out_weight[layer]
    scale = lax.rsqrt(meansq - mean * mean + EPS)
    hidden = ((values - mean) * scale * gain[:, None, None] + bias[:, None, None]).astype(
        jnp.bfloat16
    )
    update = jnp.einsum("hrn,hc->rnc", hidden, weight, preferred_element_type=jnp.float32)
    return update


def fits(pair_shape, weight_shape):
    rows, n, chan = pair_shape
    hid = weight_shape[3]
    return (
        lax.axis_size("row") == 4
        and lax.axis_size("ch") == 4
        and rows * 4 == n
        and rows <= MASK_ROWS
        and rows % 2 == 0
        and n % 8 == 0
        and n <= chan
        and hid % 16 == 0
        and hid * 4 == chan
        and chan % 128 == 0
        and n * n * chan * 4 * 6 <= 16 * 1024 * 1024
    )


def per_device(
    pair,
    chain_ids,
    mask,
    pair_embed,
    in_gain,
    in_bias,
    proj_weight,
    gate_weight,
    out_gain,
    out_bias,
    out_weight,
):
    rows = pair.shape[0]
    if fits(pair.shape, proj_weight.shape):
        return in_one_phase(
            pair, chain_ids, mask, pair_embed, in_gain, in_bias, proj_weight, gate_weight, out_gain, out_bias, out_weight
        )
    start_row = lax.axis_index("row") * rows
    own_chain = lax.dynamic_slice_in_dim(chain_ids, start_row, rows, 0)
    same = (own_chain[:, None] == chain_ids[None, :])[:, :, None]
    current = pair.astype(jnp.float32) + jnp.where(same, pair_embed[1], pair_embed[0])
    maskf = mask.astype(jnp.float32)
    result = pair
    for layer in range(2):
        normed = layer_norm(current, in_gain[layer], in_bias[layer]).astype(jnp.bfloat16)
        weights = proj_weight[layer]
        if layer == 0:
            mixed = outgoing(normed, weights, maskf)
        else:
            mixed = incoming(normed, weights, maskf)
        update = finish(mixed, layer, out_gain, out_bias, out_weight)
        gate = jax.nn.sigmoid(
            jnp.dot(normed, gate_weight[layer], preferred_element_type=jnp.float32)
        )
        result = lax.optimization_barrier((current + gate * update).astype(jnp.bfloat16))
        current = result.astype(jnp.float32)
    return result


def solution(mesh):
    placed = (
        P(("grp", "row"), None, None),
        P("grp"),
        P(("grp", "row"), None),
        P(),
        P(),
        P(),
        P(None, None, None, "ch"),
        P(),
        P(),
        P(),
        P(),
    )
    return jax.shard_map(
        per_device,
        mesh=mesh,
        in_specs=placed,
        out_specs=P(("grp", "row"), None, None),
        check_vma=False,
    )
```

```python
import functools

import jax
import jax.numpy as jnp
from jax import lax
from jax.experimental import pallas as pl
from jax.experimental.pallas import tpu as pltpu
from jax.sharding import PartitionSpec as P

EPS = 1e-05
F32 = jnp.float32
BF16 = jnp.bfloat16
MASK_ROWS = 16


def nt_dot(a, b):
    return lax.dot_general(a, b, (((1,), (1,)), ((), ())), preferred_element_type=F32)


def nn_dot(a, b):
    return lax.dot_general(a, b, (((1,), (0,)), ((), ())), preferred_element_type=F32)


def half_sigmoid(half):
    return 0.5 * jnp.tanh(half) + 0.5


def normalize(values, gain, bias):
    mean = jnp.mean(values, axis=-1, keepdims=True)
    centered = values - mean
    var = jnp.mean(centered * centered, axis=-1, keepdims=True)
    return (centered * lax.rsqrt(var + EPS) * gain + bias).astype(BF16)


def pieces(rows, most):
    out, first = [], 0
    while first < rows:
        count = min(most, rows - first)
        out.append((first, count))
        first += count
    return out


def spread_masks(mask, rows, n, chan):
    spread = (
        lax.broadcasted_iota(jnp.int32, (rows, rows * chan), 1) // chan
        == lax.broadcasted_iota(jnp.int32, (rows, rows * chan), 0)
    ).astype(BF16)
    return lax.dot_general(mask.astype(BF16), spread, (((0,), (0,)), ((), ())), preferred_element_type=F32)


def lift(pair_rows, masks, chains, embed, gain, bias, position, first, count):
    other, same = embed[0:1, :], embed[1:2, :]
    chan = chains.shape[1]
    z = jnp.concatenate(
        [
            jnp.where(chains[...] == chains[pl.ds(position + i, 1), :], same, other)
            for i in range(first, first + count)
        ],
        axis=0,
    ) + pair_rows.astype(F32)
    spread = jnp.concatenate([masks[:, i * chan : (i + 1) * chan] for i in range(first, first + count)], axis=0)
    return z, normalize(z, gain, bias), spread


def gated_side(zm, weights, u, side, chan):
    base = (u * 4 + side * 2) * chan
    both = nt_dot(zm, weights[base : base + 2 * chan, :])
    return (jnp.tanh(both[:, :chan]) + 1.0) * both[:, chan:]


def pack_kernel(n, rows, pair, mask, packed, mask_v, sems):
    block, chan = pair.shape
    copies = [
        pltpu.make_async_copy(mask, mask_v, sems.at[0]),
        pltpu.make_async_copy(pair, packed.at[pl.ds(0, block)], sems.at[1]),
    ]
    for copy in copies:
        copy.start()
    copies[0].wait()
    wide = jnp.concatenate([mask_v[...].astype(F32), jnp.zeros((rows, chan - n), F32)], axis=1)
    packed[block : block + MASK_ROWS, :] = jnp.concatenate(
        [wide, jnp.zeros((MASK_ROWS - rows, chan), F32)], axis=0
    ).astype(BF16)
    copies[1].wait()


def constants_kernel(part, packed, chain_row, *refs):
    count = (len(refs) - 4) // 2
    sources, outs = refs[:count], refs[count : 2 * count]
    chains, halved, row, sems = refs[2 * count :]
    first = pltpu.make_async_copy(chain_row, row, sems.at[count])
    first.start()
    copies = [pltpu.make_async_copy(a, b, sems.at[i]) for i, (a, b) in enumerate(zip(sources, outs))]
    for copy in copies:
        copy.start()
    core = lax.rem(lax.axis_index("ch"), 2)
    block = packed.shape[0] - MASK_ROWS
    start = pl.multiple_of(core * (block - part), 16)
    halved[0:part, :] = packed[pl.ds(start, part), :]
    halved[part : part + MASK_ROWS, :] = packed[block : block + MASK_ROWS, :]
    first.wait()
    ones = jnp.ones((1, chains.shape[1]), BF16)
    chains[...] = lax.dot_general(
        row[...].astype(F32).astype(BF16), ones, (((0,), (0,)), ((), ())), preferred_element_type=F32
    )
    for copy in copies:
        copy.wait()


def pass_kernel(value, after, out):
    out[...] = value[...]


def weights_kernel(w_o, w_e, w_a, w_f, weights):
    c = lax.axis_index("ch")
    hid = w_e.shape[0] // 8
    for at, ref in enumerate((w_o, w_e, w_a, w_f)):
        for q in range(8):
            first = pl.multiple_of(q * 4 * hid + (c ^ at) * hid, 16)
            weights[pl.ds(first, hid), :] = ref[q * hid : (q + 1) * hid, :] * jnp.asarray(0.5, BF16)


def lift_kernel(
    n, rows, which,
    packed, chains, embed, in_gain, in_bias, gate_w,
    z_ref, g_ref, m_ref, zm_ref,
):
    r = lax.axis_index("row")
    core = lax.rem(lax.axis_index("ch"), 2)
    position = (r ^ which(core)) * rows
    chan = packed.shape[1]
    masks_at = packed.shape[0] - MASK_ROWS
    masks = spread_masks(packed[masks_at : masks_at + MASK_ROWS, 0:n][0:rows], rows, n, chan)
    for first, count in pieces(rows, 8):
        at = pl.ds(first * n, count * n)
        z, zn, spread = lift(
            packed[at, :], masks, chains, embed, in_gain[0:1, :], in_bias[0:1, :], position, first, count
        )
        z_ref[at, :] = z
        m_ref[at, :] = spread
        g_ref[at, :] = half_sigmoid(0.5 * nn_dot(zn, gate_w[0]))
        zm_ref[at, :] = zn * spread.astype(BF16)


def project_kernel(n, rows, zm_ref, weights, left_ref, right_ref):
    chan = zm_ref.shape[1]
    for first, count in pieces(rows, 8):
        at = pl.ds(first * n, count * n)
        zm = zm_ref[at, :]
        left_ref[at, :] = gated_side(zm, weights, 0, 0, chan)
        right_ref[at, :] = gated_side(zm, weights, 0, 1, chan)


def tiles_of(lefts, steps, right_ref, right_at, width, right_step):
    chan = right_ref.shape[1]

    def body(k, accs):
        right = right_ref[pl.ds(pl.multiple_of(right_at + k * right_step, 8), width), :]
        return tuple(acc + ref[pl.ds(at + k * step, 1), :] * right for acc, (ref, at, step) in zip(accs, lefts))

    zeros = tuple(jnp.zeros((width, chan), F32) for _ in lefts)
    return lax.fori_loop(0, steps, body, zeros, unroll=min(28, steps))


def order_kernel(n, rows, left_o, left_a, left_e, right_o, right_a, right_e, right_ref, left_ref):
    core = lax.rem(lax.axis_index("ch"), 2)
    block, mid = rows * n, rows // 2 * n

    @pl.when(core == 0)
    def _():
        left_ref[0:block, :] = left_o[...]
        left_ref[block : block + mid, :] = left_a[0:mid, :]

    @pl.when(core == 1)
    def _():
        left_ref[0:block, :] = left_a[...]
        left_ref[block : block + mid, :] = left_e[mid:block, :]

    for j in range(rows):
        rows_of_j = slice(j * n, (j + 1) * n)
        right_ref[pl.ds(j, n, stride=n), :] = right_o[rows_of_j, :]
        right_ref[pl.ds(rows * (1 + core) + j, n, stride=n), :] = right_a[rows_of_j, :]
        right_ref[pl.ds(rows * (2 - core) + j, n, stride=n), :] = right_e[rows_of_j, :]


def early_kernel(n, rows, early, left_ref, right_ref, x_ref):
    group = rows // 2

    def some(t, _):
        first = t * group * n
        accs = tiles_of([(left_ref, first + i * n, 1) for i in range(group)], n, right_ref, 0, early, n)
        for i, acc in enumerate(accs):
            x_ref[pl.ds(pl.multiple_of(first + i * n, 8), early), :] = acc
        return 0

    lax.fori_loop(0, 3, some, 0)


def late_kernel(
    n, rows, part, early,
    half_b, half_f, weights, chains, embed, in_gain, in_bias, gate_w, out_gain, out_bias, out_w,
    x_in, right_in, left_in, z_o, z_a, z_e, g_o, g_a, g_e,
    z1_ref, own_ref, m_ref,
    x_ref, late_ref, left_ref, zn_ref, mf_ref, zf_ref,
):
    r = lax.axis_index("row")
    core = lax.rem(lax.axis_index("ch"), 2)
    even = core == 0
    block, mid = rows * n, rows // 2 * n
    chan = half_b.shape[1]
    late = n - early
    masks = spread_masks(half_b[part : part + MASK_ROWS, 0:n][0:rows], rows, n, chan)
    skip = 2 * part - block
    pair_rows = jnp.concatenate(
        [
            jnp.where(even, half_b[0:part, :], half_f[0:part, :]),
            jnp.where(even, half_f[skip:part, :], half_b[skip:part, :]),
        ],
        axis=0,
    )

    first_late = 3 * rows - early
    for t in range(first_late):
        late_ref[pl.ds(t, n, stride=late), :] = right_in[pl.ds(early + t, n, stride=n), :]
    for first, count in pieces(rows, 8):
        size = count * n
        z, zn, spread = lift(
            pair_rows[first * n : first * n + size], masks, chains, embed, in_gain[0:1, :], in_bias[0:1, :],
            (r ^ 3) * rows, first, count,
        )
        zm = zn * spread.astype(BF16)
        right = gated_side(zm, weights, 0, 1, chan)
        for j in range(count):
            late_ref[pl.ds(first_late + first + j, n, stride=late), :] = right[j * n : (j + 1) * n]
        at = pl.ds(first * n, size)
        zf_ref[at, :] = z
        mf_ref[at, :] = spread
        zn_ref[at, :] = zn.astype(F32)

    own = pl.ds(pl.multiple_of(core * mid, 8), mid)
    zn = zn_ref[own, :].astype(BF16)
    spread = mf_ref[own, :]
    left_ref[...] = gated_side(zn * spread.astype(BF16), weights, 0, 0, chan)
    m_ref[...] = spread

    group = rows // 2
    head = block + mid
    x_ref[0:head, :] = x_in[...]
    tail_lefts = [(left_ref, i * n, 1) for i in range(group)]
    for i, acc in enumerate(tiles_of(tail_lefts, n, right_in, 0, early, n)):
        x_ref[head + i * n : head + i * n + early, :] = acc
    lefts = [(left_in, i * n, 1) for i in range(3 * group)] + tail_lefts
    for t in range(2):
        for i, acc in enumerate(tiles_of(lefts[t * rows : (t + 1) * rows], n, late_ref, 0, late, late)):
            row = t * block + i * n + early
            x_ref[row : row + late, :] = acc

    def finish(first, count, z, gate):
        x = jnp.concatenate(
            [
                x_ref[pl.ds(i * n + (r ^ b) * rows, rows), :]
                for i in range(first, first + count)
                for b in range(4)
            ],
            axis=0,
        )
        update = hidden_update(x, out_gain[0:1, :], out_bias[0:1, :], out_w[0])
        z1 = (z + gate * update).astype(BF16)
        z1_ref[first * n : (first + count) * n, :] = z1.astype(F32)
        return z1

    for first, count in pieces(rows, 8):
        at = slice(first * n, (first + count) * n)
        own_ref[at, :] = finish(
            first, count, jnp.where(even, z_o[at, :], z_a[at, :]), jnp.where(even, g_o[at, :], g_a[at, :])
        )
    finish(
        rows, group,
        jnp.where(even, z_a[0:mid, :], z_e[mid:block, :]), jnp.where(even, g_a[0:mid, :], g_e[mid:block, :]),
    )
    finish(rows + group, group, zf_ref[own, :], half_sigmoid(0.5 * nn_dot(zn, gate_w[0])))


def hidden_update(x, gain, bias, weight):
    mean = jnp.mean(x, axis=-1, keepdims=True)
    meansq = jnp.mean(x * x, axis=-1, keepdims=True)
    scale = lax.rsqrt(meansq - mean * mean + EPS)
    return nn_dot(((x - mean) * scale * gain + bias).astype(BF16), weight)


def incoming_kernel(
    n, rows, z1, m_o, m_a, m_e, m_f, weights, in_gain, in_bias, part, left_ref, right_ref, sums_ref, zm_ref, own_ref
):
    r = lax.axis_index("row")
    even = lax.rem(lax.axis_index("ch"), 2) == 0
    chan = z1.shape[1]
    block, mid = rows * n, rows // 2 * n
    group = rows // 2
    kept = [
        (first, count, lambda at: jnp.where(even, m_o[at, :], m_a[at, :])) for first, count in pieces(rows, 8)
    ]
    kept.append((rows, group, lambda at: jnp.where(even, m_a[0:mid, :], m_e[mid:block, :])))
    kept.append((rows + group, group, lambda at: m_f[...]))
    for first, count, masks in kept:
        at = slice(first * n, (first + count) * n)
        zn = normalize(z1[at, :], in_gain[1:2, :], in_bias[1:2, :])
        zm = zn * masks(at).astype(BF16)
        zm_ref[at, :] = zm.astype(F32)
        right_ref[at, :] = gated_side(zm, weights, 1, 1, chan)
    for k in range(2 * rows):
        own_ref[k * rows : (k + 1) * rows, :] = zm_ref[pl.ds(k * n + r * rows, rows), :]
    left_ref[...] = gated_side(own_ref[...].astype(BF16), weights, 1, 0, chan)
    wide = (n // 8 + 1) // 2 * 8
    for t in range(2):
        for at, width in ((0, wide), (wide, n - wide)):
            accs = tiles_of([(left_ref, t * group + i, rows) for i in range(group)], 2 * rows, right_ref, at, width, n)
            for i, acc in enumerate(accs):
                row = (t * group + i) * n + at
                sums_ref[row : row + width, :] = acc
    part[...] = sums_ref[...].astype(BF16)


def gate_kernel(own, received, in_gain, in_bias, gate_w, z_ref, g_ref):
    even = lax.rem(lax.axis_index("ch"), 2) == 0
    z = jnp.where(even, own[...], received[...]).astype(F32)
    z_ref[...] = z
    zn = normalize(z, in_gain[1:2, :], in_bias[1:2, :])
    g_ref[...] = half_sigmoid(0.5 * nn_dot(zn, gate_w[1]))


def last_kernel(n, rows, part, received, z_ref, g_ref, out_gain, out_bias, out_w, result, out, sems):
    copies = []
    for first, count in pieces(rows, 8):
        at = pl.ds(first * n, count * n)
        x = part[at, :].astype(F32) + received[at, :].astype(F32)
        update = hidden_update(x, out_gain[1:2, :], out_bias[1:2, :], out_w[1])
        out[at, :] = (z_ref[at, :] + g_ref[at, :] * update).astype(BF16)
        copy = pltpu.make_async_copy(out.at[at], result.at[at], sems.at[len(copies)])
        copy.start()
        copies.append(copy)
    for copy in copies:
        copy.wait()


def in_one_phase(
    pair, chain_ids, mask, pair_embed, in_gain, in_bias, proj_weight, gate_weight, out_gain, out_bias, out_weight
):
    rows, n, chan = pair.shape
    hid = proj_weight.shape[3]
    size = 8 * hid
    block, mid = rows * n, rows // 2 * n
    flat_pair = pair.reshape(block, chan)
    weights = jnp.transpose(proj_weight, (0, 1, 3, 2)).reshape(size, chan)
    part = (block // 2 + 15) // 16 * 16
    early = 3 * rows // 8 * 8
    both = ("row", "ch")
    vmem = pl.BlockSpec(memory_space=pltpu.VMEM)

    def pairs_of(source):
        return [(source(r, c), r * 4 + c) for r in range(4) for c in range(4)]

    first = pairs_of(lambda r, c: (r ^ (1 + c % 2)) * 4 + c)
    second = pairs_of(lambda r, c: (r ^ 3) * 4 + c)
    cores = [(c, c ^ 1) for c in range(4)]
    chips = [(c, c ^ 2) for c in range(4)]

    def call(kernel, name, outs, ins, scratch=(), us=1.0):
        kept = [pltpu.with_memory_space_constraint(v, pltpu.VMEM) if id(v) in in_vmem else v for v in ins]
        got = pl.pallas_call(
            kernel,
            out_shape=tuple(outs),
            in_specs=[vmem] * len(ins),
            out_specs=tuple(vmem for _ in outs),
            scratch_shapes=[pltpu.VMEM(s, F32) for s in scratch],
            compiler_params=pltpu.CompilerParams(vmem_limit_bytes=32 * 1024 * 1024),
            cost_estimate=pl.CostEstimate(flops=int(us * 1.2e9), bytes_accessed=0, transcendentals=0),
            name=name,
        )(*kept)
        for v in got:
            in_vmem[id(v)] = v
        return got

    in_vmem = {}
    f32 = lambda count: pltpu.VMEM((count, chan), F32)
    bf16 = lambda count: pltpu.VMEM((count, chan), BF16)

    hbm = pl.BlockSpec(memory_space=pl.ANY)
    (packed,) = pl.pallas_call(
        functools.partial(pack_kernel, n, rows),
        out_shape=(bf16(block + MASK_ROWS),),
        in_specs=[hbm] * 2,
        out_specs=(vmem,),
        scratch_shapes=[pltpu.VMEM((rows, n), jnp.int32), pltpu.SemaphoreType.DMA((2,))],
        name="pack",
    )(*(pltpu.with_memory_space_constraint(v, pltpu.HBM) for v in (flat_pair, mask)))
    sources = (weights, pair_embed, in_gain, in_bias, gate_weight, out_gain, out_bias, out_weight)
    constants = pl.pallas_call(
        functools.partial(constants_kernel, part),
        out_shape=tuple(pltpu.VMEM(v.shape, v.dtype) for v in sources) + (f32(n), bf16(part + MASK_ROWS)),
        in_specs=[vmem] + [hbm] * (1 + len(sources)),
        out_specs=(vmem,) * (2 + len(sources)),
        scratch_shapes=[pltpu.VMEM((1, n), jnp.int32), pltpu.SemaphoreType.DMA((1 + len(sources),))],
        cost_estimate=pl.CostEstimate(flops=10**7, bytes_accessed=0, transcendentals=0),
        name="constants",
    )(
        pltpu.with_memory_space_constraint(packed, pltpu.VMEM),
        *(pltpu.with_memory_space_constraint(v, pltpu.HBM) for v in (chain_ids.reshape(1, n),) + sources),
    )
    in_vmem.update({id(v): v for v in (packed,) + tuple(constants)})
    w_own, pair_embed, in_gain, in_bias, gate_weight, out_gain, out_bias, out_weight, chains, halved = constants
    packed_a = lax.ppermute(packed, both, first)
    half_b = lax.ppermute(halved, both, second)
    w_e = lax.ppermute(weights, "ch", cores)
    w_a = lax.ppermute(weights, "ch", chips)
    w_f = lax.ppermute(w_a, "ch", cores)
    def one_block(name, which, source):
        return call(
            functools.partial(lift_kernel, n, rows, which),
            name,
            [f32(block)] * 3 + [bf16(block)],
            [source, chains, pair_embed, in_gain, in_bias, gate_weight],
            us=0.8,
        )

    at_o = one_block("lift_own", lambda core: 0, packed)
    (w_all,) = call(weights_kernel, "weights", [bf16(4 * size)], [w_own, w_e, w_a, w_f], us=0.1)

    def project(name, lifted):
        sides = call(functools.partial(project_kernel, n, rows), name, [f32(block)] * 2, [lifted[3], w_all], us=0.6)
        return list(lifted[:3]) + list(sides)

    (packed_a,) = call(pass_kernel, "pass_first", [bf16(block + MASK_ROWS)], [packed_a, at_o[0]], us=0.1)
    at_o = project("project_own", at_o)
    packed_e = lax.ppermute(packed_a, "ch", cores)
    at_a = one_block("lift_first", lambda core: 1 + core, packed_a)
    at_e = one_block("lift_second", lambda core: 2 - core, packed_e)
    at_a, at_e = (project(name, v) for name, v in (("project_first", at_a), ("project_second", at_e)))
    right, left = call(
        functools.partial(order_kernel, n, rows),
        "order",
        [f32(n * n), f32(block + mid)],
        [at_o[3], at_a[3], at_e[3], at_o[4], at_a[4], at_e[4]],
        us=0.3,
    )
    (half_b,) = call(pass_kernel, "pass_on", [bf16(part + MASK_ROWS)], [half_b, right], us=0.1)
    half_f = lax.ppermute(half_b, "ch", cores)
    (x,) = call(
        functools.partial(early_kernel, n, rows, early), "early", [f32(block + mid)], [left, right], us=2.0
    )
    z1, own, mask_f = call(
        functools.partial(late_kernel, n, rows, part, early),
        "late",
        [f32(2 * block), bf16(block), f32(mid)],
        [half_b, half_f, w_all, chains, pair_embed, in_gain, in_bias, gate_weight, out_gain, out_bias, out_weight]
        + [x, right, left]
        + [v[at] for at in (0, 1) for v in (at_o, at_a, at_e)],
        [(2 * block, chan), (n * (n - early), chan), (mid, chan)] + [(block, chan)] * 3,
        us=4.0,
    )
    own_n = lax.ppermute(own, "ch", cores)
    (part,) = call(
        functools.partial(incoming_kernel, n, rows),
        "incoming",
        [bf16(block)],
        [z1, at_o[2], at_a[2], at_e[2], mask_f, w_all, in_gain, in_bias],
        scratch=[(2 * rows * rows, chan), (2 * block, chan), (block, chan), (2 * block, chan), (2 * rows * rows, chan)],
        us=3.0,
    )
    part_n = lax.ppermute(part, "ch", cores)
    z1_own, gate = call(gate_kernel, "gate", [f32(block)] * 2, [own, own_n, in_gain, in_bias, gate_weight])
    result = pl.pallas_call(
        functools.partial(last_kernel, n, rows),
        out_shape=jax.ShapeDtypeStruct((block, chan), BF16),
        in_specs=[vmem] * 7,
        out_specs=hbm,
        scratch_shapes=[pltpu.VMEM((block, chan), BF16), pltpu.SemaphoreType.DMA((len(pieces(rows, 8)),))],
        compiler_params=pltpu.CompilerParams(vmem_limit_bytes=32 * 1024 * 1024),
        cost_estimate=pl.CostEstimate(flops=10**9, bytes_accessed=0, transcendentals=0),
        name="last",
    )(
        *(
            pltpu.with_memory_space_constraint(v, pltpu.VMEM) if id(v) in in_vmem else v
            for v in (part, part_n, z1_own, gate, out_gain, out_bias, out_weight)
        )
    )
    return result.reshape(rows, n, chan)


def layer_norm(values, gain, bias):
    mean = jnp.mean(values, axis=-1, keepdims=True)
    centered = values - mean
    var = jnp.mean(centered * centered, axis=-1, keepdims=True)
    return centered * lax.rsqrt(var + EPS) * gain + bias


def gated(normed, weights, maskf, form):
    proj = jnp.einsum(form, normed, weights, preferred_element_type=jnp.float32)
    return (jax.nn.sigmoid(proj[0]) * proj[1] * maskf).astype(jnp.bfloat16)


def outgoing(normed, weights, maskf):
    left = gated(normed, weights[0:2], maskf, "rnc,qch->qhrn")
    right = gated(normed, weights[2:4], maskf, "rnc,qch->qhrn")
    return jnp.einsum(
        "hik,hjk->hij",
        left,
        lax.all_gather(right, "row", axis=1, tiled=True),
        preferred_element_type=jnp.float32,
    ).astype(jnp.bfloat16)


def incoming(normed, weights, maskf):
    right = gated(normed, weights[2:4], maskf, "rnc,qch->qhrn")
    left = gated(normed, weights[0:2], maskf, "rnc,qch->qhrn")
    summed = jnp.transpose(
        lax.psum_scatter(
            jnp.einsum("hki,hkj->ihj", left, right, preferred_element_type=jnp.float32),
            "row",
            scatter_dimension=0,
            tiled=True,
        ),
        (1, 0, 2),
    )
    return summed.astype(jnp.bfloat16)


def finish(mixed, layer, out_gain, out_bias, out_weight):
    hid_full = out_weight.shape[1]
    whole = lax.all_gather(mixed, "ch", axis=0, tiled=True)
    values = whole.astype(jnp.float32)
    mean = jnp.sum(values, axis=0) / hid_full
    meansq = jnp.sum(values * values, axis=0) / hid_full
    gain = out_gain[layer]
    bias = out_bias[layer]
    weight = out_weight[layer]
    scale = lax.rsqrt(meansq - mean * mean + EPS)
    hidden = ((values - mean) * scale * gain[:, None, None] + bias[:, None, None]).astype(
        jnp.bfloat16
    )
    update = jnp.einsum("hrn,hc->rnc", hidden, weight, preferred_element_type=jnp.float32)
    return update


def fits(pair_shape, weight_shape):
    rows, n, chan = pair_shape
    hid = weight_shape[3]
    return (
        lax.axis_size("row") == 4
        and lax.axis_size("ch") == 4
        and rows * 4 == n
        and rows <= MASK_ROWS
        and rows % 2 == 0
        and n % 8 == 0
        and n <= chan
        and hid % 16 == 0
        and hid * 4 == chan
        and chan % 128 == 0
        and n * n * chan * 4 * 6 <= 16 * 1024 * 1024
    )


def per_device(
    pair,
    chain_ids,
    mask,
    pair_embed,
    in_gain,
    in_bias,
    proj_weight,
    gate_weight,
    out_gain,
    out_bias,
    out_weight,
):
    rows = pair.shape[0]
    if fits(pair.shape, proj_weight.shape):
        return in_one_phase(
            pair, chain_ids, mask, pair_embed, in_gain, in_bias, proj_weight, gate_weight, out_gain, out_bias, out_weight
        )
    start_row = lax.axis_index("row") * rows
    own_chain = lax.dynamic_slice_in_dim(chain_ids, start_row, rows, 0)
    same = (own_chain[:, None] == chain_ids[None, :])[:, :, None]
    current = pair.astype(jnp.float32) + jnp.where(same, pair_embed[1], pair_embed[0])
    maskf = mask.astype(jnp.float32)
    result = pair
    for layer in range(2):
        normed = layer_norm(current, in_gain[layer], in_bias[layer]).astype(jnp.bfloat16)
        weights = proj_weight[layer]
        if layer == 0:
            mixed = outgoing(normed, weights, maskf)
        else:
            mixed = incoming(normed, weights, maskf)
        update = finish(mixed, layer, out_gain, out_bias, out_weight)
        gate = jax.nn.sigmoid(
            jnp.dot(normed, gate_weight[layer], preferred_element_type=jnp.float32)
        )
        result = lax.optimization_barrier((current + gate * update).astype(jnp.bfloat16))
        current = result.astype(jnp.float32)
    return result


def solution(mesh):
    placed = (
        P(("grp", "row"), None, None),
        P("grp"),
        P(("grp", "row"), None),
        P(),
        P(),
        P(),
        P(None, None, None, "ch"),
        P(),
        P(),
        P(),
        P(),
    )
    return jax.shard_map(
        per_device,
        mesh=mesh,
        in_specs=placed,
        out_specs=P(("grp", "row"), None, None),
        check_vma=False,
    )
```

```python
import functools

import jax
import jax.numpy as jnp
from jax import lax
from jax.experimental import pallas as pl
from jax.experimental.pallas import tpu as pltpu
from jax.sharding import PartitionSpec as P

EPS = 1e-05
F32 = jnp.float32
BF16 = jnp.bfloat16
MASK_ROWS = 16


def nt_dot(a, b):
    return lax.dot_general(a, b, (((1,), (1,)), ((), ())), preferred_element_type=F32)


def nn_dot(a, b):
    return lax.dot_general(a, b, (((1,), (0,)), ((), ())), preferred_element_type=F32)


def half_sigmoid(half):
    return 0.5 * jnp.tanh(half) + 0.5


def normalize(values, gain, bias):
    mean = jnp.mean(values, axis=-1, keepdims=True)
    centered = values - mean
    var = jnp.mean(centered * centered, axis=-1, keepdims=True)
    return (centered * lax.rsqrt(var + EPS) * gain + bias).astype(BF16)


def pieces(rows, most):
    out, first = [], 0
    while first < rows:
        count = min(most, rows - first)
        out.append((first, count))
        first += count
    return out


def spread_masks(mask, rows, n, chan):
    spread = (
        lax.broadcasted_iota(jnp.int32, (rows, rows * chan), 1) // chan
        == lax.broadcasted_iota(jnp.int32, (rows, rows * chan), 0)
    ).astype(BF16)
    return lax.dot_general(mask.astype(BF16), spread, (((0,), (0,)), ((), ())), preferred_element_type=F32)


def lift(pair_rows, masks, chains, embed, gain, bias, position, first, count):
    other, same = embed[0:1, :], embed[1:2, :]
    chan = chains.shape[1]
    z = jnp.concatenate(
        [
            jnp.where(chains[...] == chains[pl.ds(position + i, 1), :], same, other)
            for i in range(first, first + count)
        ],
        axis=0,
    ) + pair_rows.astype(F32)
    spread = jnp.concatenate([masks[:, i * chan : (i + 1) * chan] for i in range(first, first + count)], axis=0)
    return z, normalize(z, gain, bias), spread


def gated_side(zm, weights, u, side, chan):
    base = (u * 4 + side * 2) * chan
    both = nt_dot(zm, weights[base : base + 2 * chan, :])
    return (jnp.tanh(both[:, :chan]) + 1.0) * both[:, chan:]


def pack_kernel(n, rows, pair, mask, packed, mask_v, sems):
    block, chan = pair.shape
    copies = [
        pltpu.make_async_copy(mask, mask_v, sems.at[0]),
        pltpu.make_async_copy(pair, packed.at[pl.ds(0, block)], sems.at[1]),
    ]
    for copy in copies:
        copy.start()
    copies[0].wait()
    wide = jnp.concatenate([mask_v[...].astype(F32), jnp.zeros((rows, chan - n), F32)], axis=1)
    packed[block : block + MASK_ROWS, :] = jnp.concatenate(
        [wide, jnp.zeros((MASK_ROWS - rows, chan), F32)], axis=0
    ).astype(BF16)
    copies[1].wait()


def constants_kernel(part, packed, chain_row, *refs):
    count = (len(refs) - 4) // 2
    sources, outs = refs[:count], refs[count : 2 * count]
    chains, halved, row, sems = refs[2 * count :]
    first = pltpu.make_async_copy(chain_row, row, sems.at[count])
    first.start()
    copies = [pltpu.make_async_copy(a, b, sems.at[i]) for i, (a, b) in enumerate(zip(sources, outs))]
    for copy in copies:
        copy.start()
    core = lax.rem(lax.axis_index("ch"), 2)
    block = packed.shape[0] - MASK_ROWS
    start = pl.multiple_of(core * (block - part), 16)
    halved[0:part, :] = packed[pl.ds(start, part), :]
    halved[part : part + MASK_ROWS, :] = packed[block : block + MASK_ROWS, :]
    first.wait()
    ones = jnp.ones((1, chains.shape[1]), BF16)
    chains[...] = lax.dot_general(
        row[...].astype(F32).astype(BF16), ones, (((0,), (0,)), ((), ())), preferred_element_type=F32
    )
    for copy in copies:
        copy.wait()


def pass_kernel(value, after, out):
    out[...] = value[...]


def weights_kernel(w_o, w_e, w_a, w_f, weights):
    c = lax.axis_index("ch")
    hid = w_e.shape[0] // 8
    for at, ref in enumerate((w_o, w_e, w_a, w_f)):
        for q in range(8):
            first = pl.multiple_of(q * 4 * hid + (c ^ at) * hid, 16)
            weights[pl.ds(first, hid), :] = ref[q * hid : (q + 1) * hid, :] * jnp.asarray(0.5, BF16)


def kept_from(rows, name):
    return rows // 2 // 2 * 2 if name == "second" else 0


def lift_kernel(
    n, rows, which, name,
    packed, chains, embed, in_gain, in_bias, gate_w,
    z_ref, g_ref, m_ref, zm_ref,
):
    r = lax.axis_index("row")
    core = lax.rem(lax.axis_index("ch"), 2)
    position = (r ^ which(core)) * rows
    chan = packed.shape[1]
    masks_at = packed.shape[0] - MASK_ROWS
    masks = spread_masks(packed[masks_at : masks_at + MASK_ROWS, 0:n][0:rows], rows, n, chan)
    skip = kept_from(rows, name)
    for first, count in pieces(skip, 8) + [(skip + first, count) for first, count in pieces(rows - skip, 8)]:
        at = pl.ds(first * n, count * n)
        z, zn, spread = lift(
            packed[at, :], masks, chains, embed, in_gain[0:1, :], in_bias[0:1, :], position, first, count
        )
        z_ref[at, :] = z
        m_ref[at, :] = spread
        if first >= kept_from(rows, name):
            g_ref[at, :] = half_sigmoid(0.5 * nn_dot(zn, gate_w[0]))
        zm_ref[at, :] = zn * spread.astype(BF16)


def project_kernel(n, rows, name, zm_ref, weights, left_ref, right_ref):
    chan = zm_ref.shape[1]
    skip = kept_from(rows, name)

    def left(first, count):
        at = pl.ds(first * n, count * n)
        left_ref[at, :] = gated_side(zm_ref[at, :], weights, 0, 0, chan)

    for first, count in pieces(rows, 8):
        at = pl.ds(first * n, count * n)
        right_ref[at, :] = gated_side(zm_ref[at, :], weights, 0, 1, chan)
    if name == "own":

        @pl.when(lax.rem(lax.axis_index("ch"), 2) == 0)
        def _():
            for first, count in pieces(rows, 8):
                left(first, count)

    else:
        for first, count in pieces(rows - skip, 8):
            left(skip + first, count)


def tiles_of(lefts, steps, right_ref, right_at, width, right_step):
    chan = right_ref.shape[1]

    def body(k, accs):
        right = right_ref[pl.ds(pl.multiple_of(right_at + k * right_step, 8), width), :]
        return tuple(acc + ref[pl.ds(at + k * step, 1), :] * right for acc, (ref, at, step) in zip(accs, lefts))

    zeros = tuple(jnp.zeros((width, chan), F32) for _ in lefts)
    return lax.fori_loop(0, steps, body, zeros, unroll=min(28, steps))


def order_kernel(n, rows, left_o, left_a, left_e, right_o, right_a, right_e, right_ref, left_ref):
    core = lax.rem(lax.axis_index("ch"), 2)
    block, mid = rows * n, rows // 2 * n

    @pl.when(core == 0)
    def _():
        left_ref[0:block, :] = left_o[...]
        left_ref[block : block + mid, :] = left_a[0:mid, :]

    @pl.when(core == 1)
    def _():
        left_ref[0:block, :] = left_a[...]
        left_ref[block : block + mid, :] = left_e[mid:block, :]

    for j in range(rows):
        rows_of_j = slice(j * n, (j + 1) * n)
        right_ref[pl.ds(j, n, stride=n), :] = right_o[rows_of_j, :]
        right_ref[pl.ds(rows * (1 + core) + j, n, stride=n), :] = right_a[rows_of_j, :]
        right_ref[pl.ds(rows * (2 - core) + j, n, stride=n), :] = right_e[rows_of_j, :]


def early_kernel(n, rows, early, left_ref, right_ref, x_ref):
    group = rows // 2

    def some(t, _):
        first = t * group * n
        accs = tiles_of([(left_ref, first + i * n, 1) for i in range(group)], n, right_ref, 0, early, n)
        for i, acc in enumerate(accs):
            x_ref[pl.ds(pl.multiple_of(first + i * n, 8), early), :] = acc
        return 0

    lax.fori_loop(0, 3, some, 0)


def late_kernel(
    n, rows, part, early,
    half_b, half_f, weights, chains, embed, in_gain, in_bias, gate_w, out_gain, out_bias, out_w,
    x_in, right_in, left_in, z_o, z_a, z_e, g_o, g_a, g_e,
    z1_ref, own_ref, m_ref,
    x_ref, late_ref, left_ref, zn_ref, mf_ref, zf_ref,
):
    r = lax.axis_index("row")
    core = lax.rem(lax.axis_index("ch"), 2)
    even = core == 0
    block, mid = rows * n, rows // 2 * n
    chan = half_b.shape[1]
    late = n - early
    masks = spread_masks(half_b[part : part + MASK_ROWS, 0:n][0:rows], rows, n, chan)
    skip = 2 * part - block
    pair_rows = jnp.concatenate(
        [
            jnp.where(even, half_b[0:part, :], half_f[0:part, :]),
            jnp.where(even, half_f[skip:part, :], half_b[skip:part, :]),
        ],
        axis=0,
    )

    first_late = 3 * rows - early
    for t in range(first_late):
        late_ref[pl.ds(t, n, stride=late), :] = right_in[pl.ds(early + t, n, stride=n), :]
    for first, count in pieces(rows, 8):
        size = count * n
        z, zn, spread = lift(
            pair_rows[first * n : first * n + size], masks, chains, embed, in_gain[0:1, :], in_bias[0:1, :],
            (r ^ 3) * rows, first, count,
        )
        zm = zn * spread.astype(BF16)
        right = gated_side(zm, weights, 0, 1, chan)
        for j in range(count):
            late_ref[pl.ds(first_late + first + j, n, stride=late), :] = right[j * n : (j + 1) * n]
        at = pl.ds(first * n, size)
        zf_ref[at, :] = z
        mf_ref[at, :] = spread
        zn_ref[at, :] = zn.astype(F32)

    own = pl.ds(pl.multiple_of(core * mid, 8), mid)
    zn = zn_ref[own, :].astype(BF16)
    spread = mf_ref[own, :]
    left_ref[...] = gated_side(zn * spread.astype(BF16), weights, 0, 0, chan)
    m_ref[...] = spread

    group = rows // 2
    head = block + mid
    x_ref[0:head, :] = x_in[...]
    tail_lefts = [(left_ref, i * n, 1) for i in range(group)]
    for i, acc in enumerate(tiles_of(tail_lefts, n, right_in, 0, early, n)):
        x_ref[head + i * n : head + i * n + early, :] = acc
    lefts = [(left_in, i * n, 1) for i in range(3 * group)] + tail_lefts
    for t in range(2):
        for i, acc in enumerate(tiles_of(lefts[t * rows : (t + 1) * rows], n, late_ref, 0, late, late)):
            row = t * block + i * n + early
            x_ref[row : row + late, :] = acc

    def finish(first, count, z, gate):
        x = jnp.concatenate(
            [
                x_ref[pl.ds(i * n + (r ^ b) * rows, rows), :]
                for i in range(first, first + count)
                for b in range(4)
            ],
            axis=0,
        )
        update = hidden_update(x, out_gain[0:1, :], out_bias[0:1, :], out_w[0])
        z1 = (z + gate * update).astype(BF16)
        z1_ref[first * n : (first + count) * n, :] = z1.astype(F32)
        return z1

    for first, count in pieces(rows, 8):
        at = slice(first * n, (first + count) * n)
        own_ref[at, :] = finish(
            first, count, jnp.where(even, z_o[at, :], z_a[at, :]), jnp.where(even, g_o[at, :], g_a[at, :])
        )
    finish(
        rows, group,
        jnp.where(even, z_a[0:mid, :], z_e[mid:block, :]), jnp.where(even, g_a[0:mid, :], g_e[mid:block, :]),
    )
    finish(rows + group, group, zf_ref[own, :], half_sigmoid(0.5 * nn_dot(zn, gate_w[0])))


def hidden_update(x, gain, bias, weight):
    mean = jnp.mean(x, axis=-1, keepdims=True)
    meansq = jnp.mean(x * x, axis=-1, keepdims=True)
    scale = lax.rsqrt(meansq - mean * mean + EPS)
    return nn_dot(((x - mean) * scale * gain + bias).astype(BF16), weight)


def incoming_kernel(
    n, rows, z1, m_o, m_a, m_e, m_f, weights, in_gain, in_bias, part, left_ref, right_ref, sums_ref, zm_ref, own_ref
):
    r = lax.axis_index("row")
    even = lax.rem(lax.axis_index("ch"), 2) == 0
    chan = z1.shape[1]
    block, mid = rows * n, rows // 2 * n
    group = rows // 2
    kept = [
        (first, count, lambda at: jnp.where(even, m_o[at, :], m_a[at, :])) for first, count in pieces(rows, 8)
    ]
    kept.append((rows, group, lambda at: jnp.where(even, m_a[0:mid, :], m_e[mid:block, :])))
    kept.append((rows + group, group, lambda at: m_f[...]))
    for first, count, masks in kept:
        at = slice(first * n, (first + count) * n)
        zn = normalize(z1[at, :], in_gain[1:2, :], in_bias[1:2, :])
        zm = zn * masks(at).astype(BF16)
        zm_ref[at, :] = zm.astype(F32)
        right_ref[at, :] = gated_side(zm, weights, 1, 1, chan)
    for k in range(2 * rows):
        own_ref[k * rows : (k + 1) * rows, :] = zm_ref[pl.ds(k * n + r * rows, rows), :]
    left_ref[...] = gated_side(own_ref[...].astype(BF16), weights, 1, 0, chan)
    wide = (n // 8 + 1) // 2 * 8
    for t in range(2):
        for at, width in ((0, wide), (wide, n - wide)):
            accs = tiles_of([(left_ref, t * group + i, rows) for i in range(group)], 2 * rows, right_ref, at, width, n)
            for i, acc in enumerate(accs):
                row = (t * group + i) * n + at
                sums_ref[row : row + width, :] = acc
    part[...] = sums_ref[...].astype(BF16)


def gate_kernel(own, received, in_gain, in_bias, gate_w, z_ref, g_ref):
    even = lax.rem(lax.axis_index("ch"), 2) == 0
    z = jnp.where(even, own[...], received[...]).astype(F32)
    z_ref[...] = z
    zn = normalize(z, in_gain[1:2, :], in_bias[1:2, :])
    g_ref[...] = half_sigmoid(0.5 * nn_dot(zn, gate_w[1]))


def last_kernel(n, rows, part, received, z_ref, g_ref, out_gain, out_bias, out_w, result, out, sems):
    copies = []
    for first, count in pieces(rows, 8):
        at = pl.ds(first * n, count * n)
        x = part[at, :].astype(F32) + received[at, :].astype(F32)
        update = hidden_update(x, out_gain[1:2, :], out_bias[1:2, :], out_w[1])
        out[at, :] = (z_ref[at, :] + g_ref[at, :] * update).astype(BF16)
        copy = pltpu.make_async_copy(out.at[at], result.at[at], sems.at[len(copies)])
        copy.start()
        copies.append(copy)
    for copy in copies:
        copy.wait()


def in_one_phase(
    pair, chain_ids, mask, pair_embed, in_gain, in_bias, proj_weight, gate_weight, out_gain, out_bias, out_weight
):
    rows, n, chan = pair.shape
    hid = proj_weight.shape[3]
    size = 8 * hid
    block, mid = rows * n, rows // 2 * n
    flat_pair = pair.reshape(block, chan)
    weights = jnp.transpose(proj_weight, (0, 1, 3, 2)).reshape(size, chan)
    part = (block // 2 + 15) // 16 * 16
    early = 3 * rows // 8 * 8
    both = ("row", "ch")
    vmem = pl.BlockSpec(memory_space=pltpu.VMEM)

    def pairs_of(source):
        return [(source(r, c), r * 4 + c) for r in range(4) for c in range(4)]

    first = pairs_of(lambda r, c: (r ^ (1 + c % 2)) * 4 + c)
    second = pairs_of(lambda r, c: (r ^ 3) * 4 + c)
    cores = [(c, c ^ 1) for c in range(4)]
    chips = [(c, c ^ 2) for c in range(4)]

    def call(kernel, name, outs, ins, scratch=(), us=1.0):
        kept = [pltpu.with_memory_space_constraint(v, pltpu.VMEM) if id(v) in in_vmem else v for v in ins]
        got = pl.pallas_call(
            kernel,
            out_shape=tuple(outs),
            in_specs=[vmem] * len(ins),
            out_specs=tuple(vmem for _ in outs),
            scratch_shapes=[pltpu.VMEM(s, F32) for s in scratch],
            compiler_params=pltpu.CompilerParams(vmem_limit_bytes=32 * 1024 * 1024),
            cost_estimate=pl.CostEstimate(flops=int(us * 1.2e9), bytes_accessed=0, transcendentals=0),
            name=name,
        )(*kept)
        for v in got:
            in_vmem[id(v)] = v
        return got

    in_vmem = {}
    f32 = lambda count: pltpu.VMEM((count, chan), F32)
    bf16 = lambda count: pltpu.VMEM((count, chan), BF16)

    hbm = pl.BlockSpec(memory_space=pl.ANY)
    (packed,) = pl.pallas_call(
        functools.partial(pack_kernel, n, rows),
        out_shape=(bf16(block + MASK_ROWS),),
        in_specs=[hbm] * 2,
        out_specs=(vmem,),
        scratch_shapes=[pltpu.VMEM((rows, n), jnp.int32), pltpu.SemaphoreType.DMA((2,))],
        name="pack",
    )(*(pltpu.with_memory_space_constraint(v, pltpu.HBM) for v in (flat_pair, mask)))
    sources = (weights, pair_embed, in_gain, in_bias, gate_weight, out_gain, out_bias, out_weight)
    constants = pl.pallas_call(
        functools.partial(constants_kernel, part),
        out_shape=tuple(pltpu.VMEM(v.shape, v.dtype) for v in sources) + (f32(n), bf16(part + MASK_ROWS)),
        in_specs=[vmem] + [hbm] * (1 + len(sources)),
        out_specs=(vmem,) * (2 + len(sources)),
        scratch_shapes=[pltpu.VMEM((1, n), jnp.int32), pltpu.SemaphoreType.DMA((1 + len(sources),))],
        cost_estimate=pl.CostEstimate(flops=10**7, bytes_accessed=0, transcendentals=0),
        name="constants",
    )(
        pltpu.with_memory_space_constraint(packed, pltpu.VMEM),
        *(pltpu.with_memory_space_constraint(v, pltpu.HBM) for v in (chain_ids.reshape(1, n),) + sources),
    )
    in_vmem.update({id(v): v for v in (packed,) + tuple(constants)})
    w_own, pair_embed, in_gain, in_bias, gate_weight, out_gain, out_bias, out_weight, chains, halved = constants
    packed_a = lax.ppermute(packed, both, first)
    half_b = lax.ppermute(halved, both, second)
    w_e = lax.ppermute(weights, "ch", cores)
    w_a = lax.ppermute(weights, "ch", chips)
    w_f = lax.ppermute(w_a, "ch", cores)
    def one_block(name, which, source):
        return call(
            functools.partial(lift_kernel, n, rows, which, name),
            "lift_" + name,
            [f32(block)] * 3 + [bf16(block)],
            [source, chains, pair_embed, in_gain, in_bias, gate_weight],
            us=0.8,
        )

    at_o = one_block("own", lambda core: 0, packed)
    (w_all,) = call(weights_kernel, "weights", [bf16(4 * size)], [w_own, w_e, w_a, w_f], us=0.1)

    def project(name, lifted):
        sides = call(
            functools.partial(project_kernel, n, rows, name), "project_" + name, [f32(block)] * 2, [lifted[3], w_all], us=0.6
        )
        return list(lifted[:3]) + list(sides)

    (packed_a,) = call(pass_kernel, "pass_first", [bf16(block + MASK_ROWS)], [packed_a, at_o[0]], us=0.1)
    at_o = project("own", at_o)
    packed_e = lax.ppermute(packed_a, "ch", cores)
    at_a = one_block("first", lambda core: 1 + core, packed_a)
    at_e = one_block("second", lambda core: 2 - core, packed_e)
    at_a, at_e = (project(name, v) for name, v in (("first", at_a), ("second", at_e)))
    right, left = call(
        functools.partial(order_kernel, n, rows),
        "order",
        [f32(n * n), f32(block + mid)],
        [at_o[3], at_a[3], at_e[3], at_o[4], at_a[4], at_e[4]],
        us=0.3,
    )
    (half_b,) = call(pass_kernel, "pass_on", [bf16(part + MASK_ROWS)], [half_b, right], us=0.1)
    half_f = lax.ppermute(half_b, "ch", cores)
    (x,) = call(
        functools.partial(early_kernel, n, rows, early), "early", [f32(block + mid)], [left, right], us=2.0
    )
    z1, own, mask_f = call(
        functools.partial(late_kernel, n, rows, part, early),
        "late",
        [f32(2 * block), bf16(block), f32(mid)],
        [half_b, half_f, w_all, chains, pair_embed, in_gain, in_bias, gate_weight, out_gain, out_bias, out_weight]
        + [x, right, left]
        + [v[at] for at in (0, 1) for v in (at_o, at_a, at_e)],
        [(2 * block, chan), (n * (n - early), chan), (mid, chan)] + [(block, chan)] * 3,
        us=4.0,
    )
    own_n = lax.ppermute(own, "ch", cores)
    (part,) = call(
        functools.partial(incoming_kernel, n, rows),
        "incoming",
        [bf16(block)],
        [z1, at_o[2], at_a[2], at_e[2], mask_f, w_all, in_gain, in_bias],
        scratch=[(2 * rows * rows, chan), (2 * block, chan), (block, chan), (2 * block, chan), (2 * rows * rows, chan)],
        us=3.0,
    )
    part_n = lax.ppermute(part, "ch", cores)
    z1_own, gate = call(gate_kernel, "gate", [f32(block)] * 2, [own, own_n, in_gain, in_bias, gate_weight])
    result = pl.pallas_call(
        functools.partial(last_kernel, n, rows),
        out_shape=jax.ShapeDtypeStruct((block, chan), BF16),
        in_specs=[vmem] * 7,
        out_specs=hbm,
        scratch_shapes=[pltpu.VMEM((block, chan), BF16), pltpu.SemaphoreType.DMA((len(pieces(rows, 8)),))],
        compiler_params=pltpu.CompilerParams(vmem_limit_bytes=32 * 1024 * 1024),
        cost_estimate=pl.CostEstimate(flops=10**9, bytes_accessed=0, transcendentals=0),
        name="last",
    )(
        *(
            pltpu.with_memory_space_constraint(v, pltpu.VMEM) if id(v) in in_vmem else v
            for v in (part, part_n, z1_own, gate, out_gain, out_bias, out_weight)
        )
    )
    return result.reshape(rows, n, chan)


def layer_norm(values, gain, bias):
    mean = jnp.mean(values, axis=-1, keepdims=True)
    centered = values - mean
    var = jnp.mean(centered * centered, axis=-1, keepdims=True)
    return centered * lax.rsqrt(var + EPS) * gain + bias


def gated(normed, weights, maskf, form):
    proj = jnp.einsum(form, normed, weights, preferred_element_type=jnp.float32)
    return (jax.nn.sigmoid(proj[0]) * proj[1] * maskf).astype(jnp.bfloat16)


def outgoing(normed, weights, maskf):
    left = gated(normed, weights[0:2], maskf, "rnc,qch->qhrn")
    right = gated(normed, weights[2:4], maskf, "rnc,qch->qhrn")
    return jnp.einsum(
        "hik,hjk->hij",
        left,
        lax.all_gather(right, "row", axis=1, tiled=True),
        preferred_element_type=jnp.float32,
    ).astype(jnp.bfloat16)


def incoming(normed, weights, maskf):
    right = gated(normed, weights[2:4], maskf, "rnc,qch->qhrn")
    left = gated(normed, weights[0:2], maskf, "rnc,qch->qhrn")
    summed = jnp.transpose(
        lax.psum_scatter(
            jnp.einsum("hki,hkj->ihj", left, right, preferred_element_type=jnp.float32),
            "row",
            scatter_dimension=0,
            tiled=True,
        ),
        (1, 0, 2),
    )
    return summed.astype(jnp.bfloat16)


def finish(mixed, layer, out_gain, out_bias, out_weight):
    hid_full = out_weight.shape[1]
    whole = lax.all_gather(mixed, "ch", axis=0, tiled=True)
    values = whole.astype(jnp.float32)
    mean = jnp.sum(values, axis=0) / hid_full
    meansq = jnp.sum(values * values, axis=0) / hid_full
    gain = out_gain[layer]
    bias = out_bias[layer]
    weight = out_weight[layer]
    scale = lax.rsqrt(meansq - mean * mean + EPS)
    hidden = ((values - mean) * scale * gain[:, None, None] + bias[:, None, None]).astype(
        jnp.bfloat16
    )
    update = jnp.einsum("hrn,hc->rnc", hidden, weight, preferred_element_type=jnp.float32)
    return update


def fits(pair_shape, weight_shape):
    rows, n, chan = pair_shape
    hid = weight_shape[3]
    return (
        lax.axis_size("row") == 4
        and lax.axis_size("ch") == 4
        and rows * 4 == n
        and rows <= MASK_ROWS
        and rows % 2 == 0
        and n % 8 == 0
        and n <= chan
        and hid % 16 == 0
        and hid * 4 == chan
        and chan % 128 == 0
        and n * n * chan * 4 * 6 <= 16 * 1024 * 1024
    )


def per_device(
    pair,
    chain_ids,
    mask,
    pair_embed,
    in_gain,
    in_bias,
    proj_weight,
    gate_weight,
    out_gain,
    out_bias,
    out_weight,
):
    rows = pair.shape[0]
    if fits(pair.shape, proj_weight.shape):
        return in_one_phase(
            pair, chain_ids, mask, pair_embed, in_gain, in_bias, proj_weight, gate_weight, out_gain, out_bias, out_weight
        )
    start_row = lax.axis_index("row") * rows
    own_chain = lax.dynamic_slice_in_dim(chain_ids, start_row, rows, 0)
    same = (own_chain[:, None] == chain_ids[None, :])[:, :, None]
    current = pair.astype(jnp.float32) + jnp.where(same, pair_embed[1], pair_embed[0])
    maskf = mask.astype(jnp.float32)
    result = pair
    for layer in range(2):
        normed = layer_norm(current, in_gain[layer], in_bias[layer]).astype(jnp.bfloat16)
        weights = proj_weight[layer]
        if layer == 0:
            mixed = outgoing(normed, weights, maskf)
        else:
            mixed = incoming(normed, weights, maskf)
        update = finish(mixed, layer, out_gain, out_bias, out_weight)
        gate = jax.nn.sigmoid(
            jnp.dot(normed, gate_weight[layer], preferred_element_type=jnp.float32)
        )
        result = lax.optimization_barrier((current + gate * update).astype(jnp.bfloat16))
        current = result.astype(jnp.float32)
    return result


def solution(mesh):
    placed = (
        P(("grp", "row"), None, None),
        P("grp"),
        P(("grp", "row"), None),
        P(),
        P(),
        P(),
        P(None, None, None, "ch"),
        P(),
        P(),
        P(),
        P(),
    )
    return jax.shard_map(
        per_device,
        mesh=mesh,
        in_specs=placed,
        out_specs=P(("grp", "row"), None, None),
        check_vma=False,
    )
```
